128 devices in a mesh: gx: 8 (over z, core), gy: 16 (over x, y).
Axes of the slice: x: 4, y: 4, z: 4, core: 2. Of those that a mesh axis runs over, the one named last changes fastest.
Arguments:
- leaf_up: float32 [192, 256, 456], P('gx', 'gy'), may hold values from -6 to 6
- parent_in: float32 [96, 128, 456], P('gx', 'gy'), may hold values from -6 to 6
- leaf_lists: int32 [192, 256, 40], P('gx', 'gy'), may hold values from 0 to 1, as said below
- parent_lists: int32 [96, 128, 40], P('gx', 'gy'), may hold values from 0 to 1, as said below
- up_transfer: float32 [4, 456, 456], replicated, may hold values from -0.125 to 0.125
- down_transfer: float32 [4, 456, 456], replicated, may hold values from -0.25 to 0.25
- check_inverse: float32 [456, 456], replicated, may hold values from -0.25 to 0.25
Outputs:
- leaf_down: float32 [192, 256, 456], P('gx', 'gy')
- parent_up: float32 [96, 128, 456], P('gx', 'gy')
The draws below stay inside these ranges and needn't reach their ends.
Inputs may be any that keep to these rules, and one draw needn't show every extreme that they name: `leaf_lists`: A flag is 1 only where the box at that offset lies in the grid, its parent touches or equals the box's parent, and it holds surface points. `parent_lists`: A flag is 1 only where the parent at that offset lies in the grid, its parent touches or equals the box's parent, and it holds surface points.
All inputs are finite; a program needn't handle non-finite values.
Results may differ from the reference program's by a relative error of at most 0.0001.
Values sent between devices are 32-bit elements; how exact they have to be, the bound alone decides.
A program may use at most 64 MiB of HBM per device.

```python
import math
import jax
import jax.numpy as jnp
import numpy as np
from jax import lax

ORDER = 6
DENS = 456
NX = 192
NY = 256
PX = 96
PY = 128


def offset_table_drawn():
    chosen = [(a, b) for a in range(-3, 4) for b in range(-3, 4) if max(abs(a), abs(b)) >= 2]
    return np.array(chosen, dtype=np.int32)


def occupancy(key):
    drawn = jax.random.randint(key, (NX, NY), 0, 4)
    return (drawn > 0).astype(jnp.int32)


def list_mask(occupied, row_count, col_count):
    row_place = jnp.arange(row_count, dtype=jnp.int32)[:, None]
    col_place = jnp.arange(col_count, dtype=jnp.int32)[None, :]
    columns = []
    for offset_pair in offset_table_drawn():
        source_row = row_place + int(offset_pair[0])
        source_col = col_place + int(offset_pair[1])
        inside = (source_row >= 0) & (source_row < row_count) & (source_col >= 0) & (source_col < col_count)
        nearby = (jnp.abs(source_row // 2 - row_place // 2) <= 1) & (jnp.abs(source_col // 2 - col_place // 2) <= 1)
        holder = occupied[jnp.clip(source_row, 0, row_count - 1), jnp.clip(source_col, 0, col_count - 1)]
        columns.append(jnp.where(inside & nearby, holder, 0))
    return jnp.stack(columns, axis=2).astype(jnp.int32)


def draw_leaf_lists(key, part):
    occupied = occupancy(key)
    return list_mask(occupied, NX, NY)


def draw_parent_lists(key, part):
    occupied = occupancy(key)
    parent_held = occupied.reshape(PX, 2, PY, 2).max(axis=(1, 3))
    return list_mask(parent_held, PX, PY)


def block_scale(stream_key, shape, pieces, smallest, high):
    gain = 1.0
    for dim, blocks in pieces:
        steps = jax.random.uniform(jax.random.fold_in(jax.random.fold_in(stream_key, 6), dim), (blocks,), jnp.float32, smallest / len(pieces), high / len(pieces))
        gain = gain * jnp.repeat(jnp.exp(steps), shape[dim] // blocks).reshape((-1,) + (1,) * (len(shape) - 1 - dim))
    return gain


def centred(rng, dims, scale, bound, shards=(), kind=jnp.bfloat16):
    values = jax.random.normal(rng, dims, jnp.float32) * scale
    if len(shards) > 0:
        values = block_scale(rng, dims, shards, -0.22, 0.18) * values
    return jnp.clip(values, min=-bound, max=bound).astype(kind)


def setup_inputs(seed: int = 0) -> dict:
    seeds = jax.random.split(jax.random.key(seed), 8)
    return {
        "leaf_up": centred(seeds[0], (NX, NY, DENS), 1.0, 6.0, ((0, 8), (1, 16)), jnp.float32),
        "parent_in": centred(seeds[1], (PX, PY, DENS), 1.0, 6.0, ((0, 8), (1, 16)), jnp.float32),
        "leaf_lists": draw_leaf_lists(jax.random.fold_in(seeds[7], 71), 0),
        "parent_lists": draw_parent_lists(jax.random.fold_in(seeds[7], 71), 0),
        "up_transfer": centred(seeds[4], (4, DENS, DENS), (4 * DENS) ** -0.5, 0.125, (), jnp.float32),
        "down_transfer": centred(seeds[5], (4, DENS, DENS), DENS ** -0.5, 0.25, (), jnp.float32),
        "check_inverse": centred(seeds[6], (DENS, DENS), DENS ** -0.5, 0.25, (), jnp.float32),
    }


stokes_scale = 1.0 / (8.0 * math.pi)

def offset_table():
    chosen = [(a, b) for a in range(-3, 4) for b in range(-3, 4) if max(abs(a), abs(b)) >= 2]
    return np.array(chosen, dtype=np.int32)

def surface_points():
    grid_line = np.linspace(-1.0, 1.0, ORDER)
    points = []
    for i in range(ORDER):
        for j in range(ORDER):
            for k in range(ORDER):
                if min(i, j, k) == 0 or max(i, j, k) == ORDER - 1:
                    points.append((grid_line[i], grid_line[j], grid_line[k]))
    return np.array(points, dtype=np.float32).T

def kernel_matrix(shift_row, shift_col):
    surface = surface_points()
    spacing = 0.525 * (surface[:, :, None] - surface[:, None, :])
    components = (jnp.asarray(spacing[0]) - shift_row, jnp.asarray(spacing[1]) - shift_col, jnp.asarray(spacing[2]) + 0.0 * shift_row)
    squared = components[0] * components[0] + components[1] * components[1] + components[2] * components[2]
    inverse = 1.0 / jnp.sqrt(squared)
    cubed = inverse * inverse * inverse
    blocks = []
    for a in range(3):
        line_blocks = []
        for b in range(3):
            entry = components[a] * components[b] * cubed
            if a == b:
                entry = entry + inverse
            line_blocks.append(entry * stokes_scale)
        blocks.append(jnp.concatenate(line_blocks, axis=1))
    return jnp.concatenate(blocks, axis=0)

def interact(padded, lists, row_count, col_count):
    features = padded.shape[2]
    offsets = jnp.asarray(offset_table()).reshape(10, 4, 2)
    picks = jnp.arange(40, dtype=jnp.int32).reshape(10, 4)

    def advance(running, cluster):
        pairs_now, picks_now = cluster
        sources = []
        matrices = []
        for member in range(4):
            offset_pair = pairs_now[member]
            source = lax.dynamic_slice(padded, (offset_pair[0] + 3, offset_pair[1] + 3, jnp.int32(0)), (row_count, col_count, features))
            weight = lax.dynamic_slice_in_dim(lists, picks_now[member], 1, 2).astype(jnp.float32)
            sources.append((source * weight).reshape(row_count * col_count, features))
            matrices.append(kernel_matrix(offset_pair[0].astype(jnp.float32), offset_pair[1].astype(jnp.float32)))
        stacked_source = jnp.concatenate(sources, axis=1)
        stacked_matrix = jnp.concatenate(matrices, axis=1)
        product = lax.dot_general(stacked_source, stacked_matrix, (((1,), (1,)), ((), ())), precision=lax.Precision.HIGHEST, preferred_element_type=jnp.float32)
        return (running + product, None)
    start = jnp.zeros((row_count * col_count, features), jnp.float32)
    running, _ = lax.scan(advance, start, (offsets, picks))
    return running

def gather_children(leaf_values, up_transfer):
    row_count, col_count, features = leaf_values.shape
    grouped = leaf_values.reshape(row_count // 2, 2, col_count // 2, 2, features)
    operators = up_transfer.reshape(2, 2, features, features)
    return jnp.einsum('acbdk,cdjk->abj', grouped, operators, precision=lax.Precision.HIGHEST)

def spread_children(parent_values, down_transfer):
    row_count, col_count, features = parent_values.shape
    operators = down_transfer.reshape(2, 2, features, features)
    spread = jnp.einsum('abk,cdjk->acbdj', parent_values, operators, precision=lax.Precision.HIGHEST)
    return spread.reshape(2 * row_count, 2 * col_count, features)

def apply_inverse(check_values, check_inverse):
    return lax.dot_general(check_values, check_inverse, (((1,), (1,)), ((), ())), precision=lax.Precision.HIGHEST, preferred_element_type=jnp.float32)

def reference(leaf_up, parent_in, leaf_lists, parent_lists, up_transfer, down_transfer, check_inverse):
    features = leaf_up.shape[2]
    parent_up = gather_children(leaf_up, up_transfer)
    parent_padded = jnp.pad(parent_up, ((3, 3), (3, 3), (0, 0)))
    parent_check = interact(parent_padded, parent_lists, PX, PY)
    parent_local = parent_in + apply_inverse(parent_check, check_inverse).reshape(PX, PY, features)
    leaf_padded = jnp.pad(leaf_up, ((3, 3), (3, 3), (0, 0)))
    leaf_check = interact(leaf_padded, leaf_lists, NX, NY).reshape(NX, NY, features)
    leaf_check = leaf_check + spread_children(parent_local, down_transfer)
    leaf_down = apply_inverse(leaf_check.reshape(NX * NY, features), check_inverse).reshape(NX, NY, features)
    return (leaf_down, parent_up)
```

```python
import functools
import itertools

import jax
import jax.numpy as jnp
import ml_dtypes
import numpy as np
from jax import lax
from jax.experimental import pallas as pl
from jax.experimental.pallas import tpu as pltpu
from jax.sharding import PartitionSpec as P

ORDER = 6
DENS = 456
TOP = 14
F32 = jnp.float32
BF16 = jnp.bfloat16
MESH = pl.DeviceIdType.MESH

ALL_OFFSETS = [(a, b) for a in range(-3, 4) for b in range(-3, 4) if max(abs(a), abs(b)) >= 2]
EVEN_OFFSETS = [(a, b) for a in range(-2, 4) for b in range(-2, 4) if max(abs(a), abs(b)) >= 2]
COUNT = len(EVEN_OFFSETS)


def rounded(values):
    return values.astype(ml_dtypes.bfloat16).astype(np.float64)


def surface_points():
    grid_line = np.linspace(-1.0, 1.0, ORDER)
    points = []
    for i in range(ORDER):
        for j in range(ORDER):
            for k in range(ORDER):
                if min(i, j, k) == 0 or max(i, j, k) == ORDER - 1:
                    points.append((grid_line[i], grid_line[j], grid_line[k]))
    return np.array(points)


def kernel_matrix(points, shift):
    r = 0.525 * (points[:, None, :] - points[None, :, :]) - np.array([shift[0], shift[1], 0.0])
    length = np.sqrt((r * r).sum(-1))
    count = len(points)
    matrix = np.zeros((3, count, 3, count))
    for a in range(3):
        for b in range(3):
            matrix[a, :, b, :] = (float(a == b) / length + r[..., a] * r[..., b] / length**3) / (8.0 * np.pi)
    return matrix.reshape(3 * count, 3 * count)


def mirror_basis(points, signs):
    count = len(points)
    place = {tuple(np.round(p * (ORDER - 1)).astype(int)): i for i, p in enumerate(points)}
    corner = [i for i, p in enumerate(points) if (p > 0).all()]
    basis = np.zeros((3 * count, 3 * len(corner)))
    for a in range(3):
        for h, i in enumerate(corner):
            for flip in itertools.product([1, -1], repeat=3):
                j = place[tuple(np.round(points[i] * np.array(flip) * (ORDER - 1)).astype(int))]
                sign = 1
                for axis in range(3):
                    if flip[axis] == -1:
                        sign *= signs[axis] * (-1 if axis == a else 1)
                basis[a * count + j, a * len(corner) + h] = sign
    return basis / np.sqrt(8.0)


@functools.lru_cache(maxsize=1)
def tables():
    points = surface_points()
    kernels = {o: kernel_matrix(points, o) for o in ALL_OFFSETS}
    stacked = np.concatenate([kernels[o] for o in ALL_OFFSETS], axis=1)
    basis = np.zeros((DENS, 512))
    sign_y = np.ones(512)
    high, low, main = [], [], []
    for t, (sx, sz) in enumerate([(1, 1), (-1, 1), (1, -1), (-1, -1)]):
        found = []
        for sy in (1, -1):
            mirror = mirror_basis(points, (sx, sy, sz))
            left, size, _ = np.linalg.svd(mirror.T @ stacked, full_matrices=False)
            for j in range(left.shape[1]):
                found.append((size[j], sy, rounded(mirror @ left[:, j])))
        found.sort(key=lambda item: -item[0])
        start = 128 * t + 32 * t
        special = range(start, start + 2 * TOP)
        rest = [lane for lane in range(128 * t, 128 * t + 128) if lane not in special]
        for j, (_, sy, column) in enumerate(found):
            lane = start + j if j < TOP else rest[j - TOP]
            basis[:, lane] = column
            sign_y[lane] = sy
            main.append(lane)
            if j < TOP:
                high.append(lane)
                low.append(lane + TOP)
                sign_y[lane + TOP] = sy
    inverse = np.linalg.inv(basis[:, main])
    doubled = basis.copy()
    doubled[:, low] = basis[:, high]
    special = np.zeros((DENS, 128))
    for t in range(4):
        special[:, 32 * t : 32 * t + 2 * TOP] = doubled[:, 160 * t : 160 * t + 2 * TOP]
    weights = np.zeros((2, COUNT, 256, 256), ml_dtypes.bfloat16)
    for k, offset in enumerate(EVEN_OFFSETS):
        core = np.zeros((512, 512))
        core[np.ix_(main, main)] = (inverse @ kernels[offset] @ inverse.T).T
        leading = core[np.ix_(high, high)]
        core[np.ix_(low, high)] = leading
        core[np.ix_(high, low)] = leading - rounded(leading)
        weights[0, k] = core[:256, :256].astype(ml_dtypes.bfloat16)
        weights[1, k] = core[256:, 256:].astype(ml_dtypes.bfloat16)
    picks = np.zeros((2, 2, len(ALL_OFFSETS), 128), ml_dtypes.bfloat16)
    for cx in range(2):
        for cy in range(2):
            for k, (a, b) in enumerate(EVEN_OFFSETS):
                offset = (-a if cx else a, -b if cy else b)
                picks[cx, cy, ALL_OFFSETS.index(offset), k] = 1
    return {
        "weights": weights.reshape(2, COUNT * 256, 256),
        "doubled": doubled.astype(ml_dtypes.bfloat16),
        "special": special.astype(ml_dtypes.bfloat16),
        "doubled_t": np.ascontiguousarray(doubled.T).astype(ml_dtypes.bfloat16),
        "special_t": np.ascontiguousarray(special.T).astype(ml_dtypes.bfloat16),
        "sign_y": np.tile(sign_y[None, :], (8, 1)).astype(np.float32),
        "picks": picks,
    }


def split(value):
    high = value.astype(BF16)
    return high, (value - high.astype(F32)).astype(BF16)


def mm(a, b):
    return jnp.dot(a, b, preferred_element_type=F32)


def mm_t(a, b):
    return lax.dot_general(a, b, (((1,), (1,)), ((), ())), preferred_element_type=F32)


def product(rows, matrix):
    rh, rl = rows
    mh, ml = matrix
    return mm_t(rh, mh) + mm_t(rl, mh) + mm_t(rh, ml)


def lanes(t):
    return slice(128 * t, 128 * t + 128)


def lane_index(shape):
    return lax.broadcasted_iota(jnp.int32, shape, len(shape) - 1)


def project(rows, doubled, special):
    high, low = split(rows)
    main = mm(high, doubled)
    fine = mm(low, special)
    place = lane_index(fine.shape)
    tiles = []
    for t in range(4):
        tile = main[:, lanes(t)]
        tile = jnp.where((place >= 32 * t) & (place < 32 * t + 32), tile + fine, tile)
        left_over = tile - tile.astype(BF16).astype(F32)
        tiles.append(jnp.where((place >= 32 * t + TOP) & (place < 32 * t + 2 * TOP), left_over, tile))
    return jnp.concatenate(tiles, axis=1)


def expand(y, doubled_t, special_t):
    high = y.astype(BF16)
    rest = y - high.astype(F32)
    place = lane_index((y.shape[0], 128))
    fine = jnp.zeros((y.shape[0], 128), F32)
    for t in range(4):
        fine = jnp.where((place >= 32 * t) & (place < 32 * t + 32), rest[:, lanes(t)], fine)
    return mm(high, doubled_t) + mm(fine.astype(BF16), special_t)


def build_shifts(padded, shifted, sign_y, width):
    blocks = padded.shape[1]
    row = lax.broadcasted_iota(jnp.int32, (blocks, width, 512), 1)
    even = lax.rem(row, 2) == 0
    signs = sign_y[0:1, :].reshape(1, 1, 512)
    for d in range(6):
        step = d - 2
        for parity in range(2):
            forward = padded[parity, :, 8 + step : 8 + step + width, :]
            backward = padded[parity, :, 8 - step : 8 - step + width, :] * signs
            shifted[d, parity] = jnp.where(even, forward, backward).astype(shifted.dtype)


def interact(shifted, lists, picks, sign_y, weights, total, half, width, group):
    count = half * width
    flags = []
    for cx in range(2):
        found = []
        for x in range(1):
            block = lists[cx].astype(F32).reshape(count, len(ALL_OFFSETS)).astype(BF16)
            found = [mm(block, picks[cx, cy]).reshape(half, width, 128) for cy in range(2)]
        row = lax.broadcasted_iota(jnp.int32, (half, width, 128), 1)
        flags.append(jnp.where(lax.rem(row, 2) == 0, found[0], found[1]))
    for first in range(0, COUNT, group):
        parts = [[], []]
        for k in range(first, min(first + group, COUNT)):
            a, b = EVEN_OFFSETS[k]
            pieces = [[] for _ in range(4)]
            for cx in range(2):
                source = cx + (-a if cx else a)
                parity, start = source % 2, source // 2 + 1
                flag = jnp.broadcast_to(flags[cx][:, :, k : k + 1], (half, width, 128)).astype(shifted.dtype)
                for t in range(4):
                    mask = -flag if (cx and t % 2) else flag
                    piece = shifted[b + 2, parity, start : start + half, :, lanes(t)] * mask
                    pieces[t].append(piece.reshape(count, 128).astype(BF16))
            for t in range(4):
                parts[t // 2].append(jnp.concatenate(pieces[t], axis=0))
        last = min(first + group, COUNT)
        for z in range(2):
            left = jnp.concatenate(parts[z], axis=1)
            term = mm(left, weights[z, first * 256 : last * 256, :])
            cols = slice(256 * z, 256 * z + 256)
            if first == 0:
                total[:, cols] = term
            else:
                total[:, cols] += term


def resigned(y, sign_y, cx, half, width):
    row = lax.broadcasted_iota(jnp.int32, (half, width, 512), 1)
    signs = sign_y[0:1, :].reshape(1, 1, 512)
    place = lane_index((1, 1, 512))
    if cx:
        turn = jnp.where(lax.rem(lax.div(place, 128), 2) == 1, -1.0, 1.0)
        return jnp.where(lax.rem(row, 2) == 0, y * turn, y * (signs * turn))
    return jnp.where(lax.rem(row, 2) == 0, y, y * signs)


DIRECTIONS = [(-1, 0), (1, 0), (0, -1), (0, 1), (-1, -1), (-1, 1), (1, -1), (1, 1)]


def pack_sides(block, strips, corners, rows, width):
    half = rows // 2
    for side in range(2):
        for col in range(2):
            y = (width - 2 if side else 0) + col
            for parity in range(2):
                for i in range(half):
                    at = parity * half + i
                    strips[side, col, at : at + 1, :] = block[2 * i + parity, y : y + 1, :]
    corners[...] = jnp.zeros_like(corners)
    for sx in range(2):
        for sy in range(2):
            for col in range(2):
                y = (width - 2 if sy else 0) + col
                for parity in range(2):
                    x = (rows - 2 if sx else 0) + parity
                    at = 2 * col + parity
                    corners[sx, sy, at : at + 1, :] = block[x, y : y + 1, :]


def side_copies(block, strips, corners, got_x, got_y, got_c, send, recv, rows, ids):
    copies = []
    for n, (dx, dy) in enumerate(DIRECTIONS):
        sx, sy = (dx + 1) // 2, (dy + 1) // 2
        if dy == 0:
            source = block.at[rows - 2 : rows] if dx > 0 else block.at[0:2]
            target = got_x.at[1 - sx]
        elif dx == 0:
            source, target = strips.at[sy], got_y.at[1 - sy]
        else:
            source, target = corners.at[sx, sy], got_c.at[1 - sx, 1 - sy]
        copies.append(
            pltpu.make_async_remote_copy(
                src_ref=source,
                dst_ref=target,
                send_sem=send.at[n],
                recv_sem=recv.at[n],
                device_id=ids[n],
                device_id_type=MESH,
            )
        )
    return copies


def fill(padded, local, got_x, got_y, got_c, held, doubled, special, rows, width, strip, chunk):
    half = rows // 2
    for c in range(0, half, chunk):
        value = local[2 * c : 2 * c + 2 * chunk].reshape(2 * chunk * width, DENS)
        value = project(value, doubled, special).reshape(chunk, 2, width, 512)
        for parity in range(2):
            padded[parity, 1 + c : 1 + c + chunk, 8 : 8 + width, :] = value[:, parity]


def fill_sides(padded, got_x, got_y, got_c, held, doubled, special, rows, width, strip):
    half = rows // 2
    value = project(got_x[...].reshape(4 * width, DENS), doubled, special).reshape(2, 2, width, 512)
    for side in range(2):
        for parity in range(2):
            padded[parity, (half + 1) * side, 8 : 8 + width, :] = value[side, parity]
    value = project(got_y[...].reshape(4 * strip, DENS), doubled, special)
    held[0 : 4 * strip, :] = value
    value = project(got_c[...].reshape(32, DENS), doubled, special)
    held[4 * strip : 4 * strip + 32, :] = value
    zero = jnp.zeros((half + 2, 8, 512), F32)
    for parity in range(2):
        padded[parity, :, 0:8, :] = zero
        padded[parity, :, 8 + width : 16 + width, :] = zero
    for side in range(2):
        for col in range(2):
            y = 8 + width + col if side else 6 + col
            for parity in range(2):
                for i in range(half):
                    at = (side * 2 + col) * strip + parity * half + i
                    padded[parity, 1 + i, y : y + 1, :] = held[at : at + 1, :]
                for sx in range(2):
                    at = 4 * strip + (sx * 2 + side) * 8 + 2 * col + parity
                    padded[parity, (half + 1) * sx, y : y + 1, :] = held[at : at + 1, :]


def body(
    sizes,
    leaf_hbm, parent_in_hbm, leaf_lists_hbm, parent_lists_hbm, up_hbm, down_hbm, inverse_hbm,
    weights_hbm, doubled_hbm, special_hbm, doubled_t_hbm, special_t_hbm, sign_hbm, picks_hbm,
    leaf_down_hbm, parent_up_hbm,
    leaf, parent_in, leaf_lists, parent_lists, up, down, inverse,
    weights, doubled, special, doubled_t, special_t, sign_y, picks,
    leaf_strips, leaf_corners, leaf_got_x, leaf_got_y, leaf_got_c, leaf_held, leaf_padded, leaf_shifted, leaf_total, leaf_check,
    parent_up, parent_strips, parent_corners, parent_got_x, parent_got_y, parent_got_c, parent_held, parent_padded,
    parent_shifted, parent_total, parent_local,
    load_sem, out_sem, leaf_send, leaf_recv, parent_send, parent_recv,
):
    rows, width, prows, pwidth, gx_size, gy_size = sizes
    half, phalf = rows // 2, prows // 2
    gx, gy = lax.axis_index("gx"), lax.axis_index("gy")
    ids = [
        (lax.rem(gx + dx + gx_size, gx_size), lax.rem(gy + dy + gy_size, gy_size)) for dx, dy in DIRECTIONS
    ]
    barrier = pltpu.get_barrier_semaphore()
    for place in ids:
        pl.semaphore_signal(barrier, inc=1, device_id=place, device_id_type=MESH)

    pairs = [(leaf_hbm, leaf)]
    pairs += [(up_hbm.at[c], up.at[c]) for c in range(4)]
    pairs += [(doubled_hbm, doubled), (special_hbm, special), (sign_hbm, sign_y), (picks_hbm, picks)]
    pairs += [(leaf_lists_hbm, leaf_lists), (weights_hbm, weights)]
    pairs += [(doubled_t_hbm, doubled_t), (special_t_hbm, special_t)]
    pairs += [(parent_lists_hbm, parent_lists), (inverse_hbm, inverse), (parent_in_hbm, parent_in), (down_hbm, down)]
    loads = [pltpu.make_async_copy(a, b, load_sem.at[n]) for n, (a, b) in enumerate(pairs)]
    for load in loads:
        load.start()

    loads[0].wait()
    pack_sides(leaf, leaf_strips, leaf_corners, rows, width)
    pl.semaphore_wait(barrier, len(DIRECTIONS))
    leaf_copies = side_copies(
        leaf, leaf_strips, leaf_corners, leaf_got_x, leaf_got_y, leaf_got_c, leaf_send, leaf_recv, rows, ids
    )
    for copy in leaf_copies:
        copy.start()

    total = jnp.zeros((phalf * 2 * pwidth, DENS), F32)
    for c in range(4):
        loads[1 + c].wait()
        child = leaf[...].reshape(prows, 2, width, DENS)[:, c // 2]
        child = child.reshape(prows, pwidth, 2, DENS)[:, :, c % 2, :].reshape(prows * pwidth, DENS)
        total = total + product(split(child), split(up[c]))
    parent_up[...] = total.reshape(prows, pwidth, DENS)
    parent_out = pltpu.make_async_copy(parent_up, parent_up_hbm, out_sem.at[0])
    parent_out.start()
    pack_sides(parent_up, parent_strips, parent_corners, prows, pwidth)
    parent_copies = side_copies(
        parent_up, parent_strips, parent_corners, parent_got_x, parent_got_y, parent_got_c,
        parent_send, parent_recv, prows, ids,
    )
    for copy in parent_copies:
        copy.start()

    for load in loads[5:10]:
        load.wait()
    fill(leaf_padded, leaf, None, None, None, None, doubled[...], special[...], rows, width, None, 3)
    for copy in leaf_copies:
        copy.wait()
    fill_sides(leaf_padded, leaf_got_x, leaf_got_y, leaf_got_c, leaf_held, doubled[...], special[...], rows, width, rows)
    build_shifts(leaf_padded, leaf_shifted, sign_y, width)
    loads[10].wait()
    loads[11].wait()
    loads[12].wait()
    lists = leaf_lists[...].reshape(half, 2, width, len(ALL_OFFSETS))
    interact(leaf_shifted, [lists[:, 0], lists[:, 1]], picks, sign_y, weights, leaf_total, half, width, 3)
    for cx in range(2):
        for c in range(0, half, 3):
            at = (cx * half + c) * width
            y = leaf_total[at : at + 3 * width, :].reshape(3, width, 512)
            y = resigned(y, sign_y, cx, 3, width).reshape(3 * width, 512)
            value = expand(y, doubled_t[...], special_t[...]).reshape(3, width, DENS)
            for i in range(3):
                leaf_check[2 * (c + i) + cx] = value[i]

    fill(parent_padded, parent_up, None, None, None, None, doubled[...], special[...], prows, pwidth, None, 6)
    for copy in parent_copies:
        copy.wait()
    fill_sides(
        parent_padded, parent_got_x, parent_got_y, parent_got_c, parent_held, doubled[...], special[...], prows, pwidth, 16
    )
    build_shifts(parent_padded, parent_shifted, sign_y, pwidth)
    for load in loads[13:]:
        load.wait()
    lists = parent_lists[...].reshape(phalf, 2, pwidth, len(ALL_OFFSETS))
    interact(parent_shifted, [lists[:, 0], lists[:, 1]], picks, sign_y, weights, parent_total, phalf, pwidth, 3)
    inverse_pair = split(inverse[...])
    for cx in range(2):
        at = cx * phalf * pwidth
        y = parent_total[at : at + phalf * pwidth, :].reshape(phalf, pwidth, 512)
        y = resigned(y, sign_y, cx, phalf, pwidth).reshape(phalf * pwidth, 512)
        value = product(split(expand(y, doubled_t[...], special_t[...])), inverse_pair).reshape(phalf, pwidth, DENS)
        for i in range(phalf):
            parent_local[2 * i + cx] = value[i] + parent_in[2 * i + cx]
    local = split(parent_local[...].reshape(prows * pwidth, DENS))
    for cx in range(2):
        sides = []
        for cy in range(2):
            sides.append(product(local, split(down[2 * cx + cy])).reshape(prows, pwidth, 1, DENS))
        both = jnp.concatenate(sides, axis=2).reshape(prows, width, DENS)
        for i in range(prows):
            leaf_check[2 * i + cx] += both[i]
    outs = []
    for c in range(4):
        at = 6 * c
        value = leaf_check[at : at + 6].reshape(6 * width, DENS)
        leaf_check[at : at + 6] = product(split(value), inverse_pair).reshape(6, width, DENS)
        out = pltpu.make_async_copy(leaf_check.at[at : at + 6], leaf_down_hbm.at[at : at + 6], out_sem.at[1 + c])
        out.start()
        outs.append(out)
    parent_out.wait()
    for out in outs:
        out.wait()


def local(sizes, leaf_up, parent_in, leaf_lists, parent_lists, up_transfer, down_transfer, check_inverse):
    rows, width, prows, pwidth = sizes[:4]
    half, phalf = rows // 2, prows // 2
    names = ("weights", "doubled", "special", "doubled_t", "special_t", "sign_y", "picks")
    constants = [jnp.asarray(tables()[name]) for name in names]
    operands = [leaf_up, parent_in, leaf_lists, parent_lists, up_transfer, down_transfer, check_inverse] + constants
    scratch = [pltpu.VMEM(x.shape, x.dtype) for x in operands]

    def sides(rows_here, width_here, strip):
        return [
            pltpu.VMEM((2, 2, strip, DENS), F32),
            pltpu.VMEM((2, 2, 8, DENS), F32),
            pltpu.VMEM((2, 2, width_here, DENS), F32),
            pltpu.VMEM((2, 2, strip, DENS), F32),
            pltpu.VMEM((2, 2, 8, DENS), F32),
            pltpu.VMEM((4 * strip + 32, 512), F32),
            pltpu.VMEM((2, rows_here // 2 + 2, 16 + width_here, 512), F32),
        ]

    scratch += sides(rows, width, rows)
    scratch += [
        pltpu.VMEM((6, 2, half + 2, width, 512), BF16),
        pltpu.VMEM((rows * width, 512), F32),
        pltpu.VMEM((rows, width, DENS), F32),
        pltpu.VMEM((prows, pwidth, DENS), F32),
    ]
    scratch += sides(prows, pwidth, 16)
    scratch += [
        pltpu.VMEM((6, 2, phalf + 2, pwidth, 512), F32),
        pltpu.VMEM((prows * pwidth, 512), F32),
        pltpu.VMEM((prows, pwidth, DENS), F32),
        pltpu.SemaphoreType.DMA((17,)),
        pltpu.SemaphoreType.DMA((5,)),
        pltpu.SemaphoreType.DMA((8,)),
        pltpu.SemaphoreType.DMA((8,)),
        pltpu.SemaphoreType.DMA((8,)),
        pltpu.SemaphoreType.DMA((8,)),
    ]
    return pl.pallas_call(
        functools.partial(body, sizes),
        out_shape=(
            jax.ShapeDtypeStruct((rows, width, DENS), F32),
            jax.ShapeDtypeStruct((prows, pwidth, DENS), F32),
        ),
        in_specs=[pl.BlockSpec(memory_space=pl.ANY)] * len(operands),
        out_specs=(pl.BlockSpec(memory_space=pl.ANY),) * 2,
        scratch_shapes=scratch,
        compiler_params=pltpu.CompilerParams(
            collective_id=0, has_side_effects=True, vmem_limit_bytes=56 * 1024 * 1024
        ),
    )(*operands)


def solution(mesh):
    gx_size, gy_size = mesh.shape["gx"], mesh.shape["gy"]
    sizes = (192 // gx_size, 256 // gy_size, 96 // gx_size, 128 // gy_size, gx_size, gy_size)
    placed = (P("gx", "gy", None),) * 4 + (P(), P(), P())
    return jax.shard_map(
        functools.partial(local, sizes),
        mesh=mesh,
        in_specs=placed,
        out_specs=(P("gx", "gy", None), P("gx", "gy", None)),
        check_vma=False,
    )
```

```python
import functools
import itertools

import jax
import jax.numpy as jnp
import ml_dtypes
import numpy as np
from jax import lax
from jax.experimental import pallas as pl
from jax.experimental.pallas import tpu as pltpu
from jax.sharding import PartitionSpec as P

ORDER = 6
DENS = 456
TOP = 14
F32 = jnp.float32
BF16 = jnp.bfloat16
MESH = pl.DeviceIdType.MESH

ALL_OFFSETS = [(a, b) for a in range(-3, 4) for b in range(-3, 4) if max(abs(a), abs(b)) >= 2]
EVEN_OFFSETS = [(a, b) for a in range(-2, 4) for b in range(-2, 4) if max(abs(a), abs(b)) >= 2]
COUNT = len(EVEN_OFFSETS)


def rounded(values):
    return values.astype(ml_dtypes.bfloat16).astype(np.float64)


def surface_points():
    grid_line = np.linspace(-1.0, 1.0, ORDER)
    points = []
    for i in range(ORDER):
        for j in range(ORDER):
            for k in range(ORDER):
                if min(i, j, k) == 0 or max(i, j, k) == ORDER - 1:
                    points.append((grid_line[i], grid_line[j], grid_line[k]))
    return np.array(points)


def kernel_matrix(points, shift):
    r = 0.525 * (points[:, None, :] - points[None, :, :]) - np.array([shift[0], shift[1], 0.0])
    length = np.sqrt((r * r).sum(-1))
    count = len(points)
    matrix = np.zeros((3, count, 3, count))
    for a in range(3):
        for b in range(3):
            matrix[a, :, b, :] = (float(a == b) / length + r[..., a] * r[..., b] / length**3) / (8.0 * np.pi)
    return matrix.reshape(3 * count, 3 * count)


def mirror_basis(points, signs):
    count = len(points)
    place = {tuple(np.round(p * (ORDER - 1)).astype(int)): i for i, p in enumerate(points)}
    corner = [i for i, p in enumerate(points) if (p > 0).all()]
    basis = np.zeros((3 * count, 3 * len(corner)))
    for a in range(3):
        for h, i in enumerate(corner):
            for flip in itertools.product([1, -1], repeat=3):
                j = place[tuple(np.round(points[i] * np.array(flip) * (ORDER - 1)).astype(int))]
                sign = 1
                for axis in range(3):
                    if flip[axis] == -1:
                        sign *= signs[axis] * (-1 if axis == a else 1)
                basis[a * count + j, a * len(corner) + h] = sign
    return basis / np.sqrt(8.0)


@functools.lru_cache(maxsize=1)
def tables():
    points = surface_points()
    kernels = {o: kernel_matrix(points, o) for o in ALL_OFFSETS}
    stacked = np.concatenate([kernels[o] for o in ALL_OFFSETS], axis=1)
    basis = np.zeros((DENS, 512))
    sign_y = np.ones(512)
    high, low, main = [], [], []
    for t, (sx, sz) in enumerate([(1, 1), (-1, 1), (1, -1), (-1, -1)]):
        found = []
        for sy in (1, -1):
            mirror = mirror_basis(points, (sx, sy, sz))
            left, size, _ = np.linalg.svd(mirror.T @ stacked, full_matrices=False)
            for j in range(left.shape[1]):
                found.append((size[j], sy, rounded(mirror @ left[:, j])))
        found.sort(key=lambda item: -item[0])
        start = 128 * t + 32 * t
        special = range(start, start + 2 * TOP)
        rest = [lane for lane in range(128 * t, 128 * t + 128) if lane not in special]
        for j, (_, sy, column) in enumerate(found):
            lane = start + j if j < TOP else rest[j - TOP]
            basis[:, lane] = column
            sign_y[lane] = sy
            main.append(lane)
            if j < TOP:
                high.append(lane)
                low.append(lane + TOP)
                sign_y[lane + TOP] = sy
    inverse = np.linalg.inv(basis[:, main])
    doubled = basis.copy()
    doubled[:, low] = basis[:, high]
    special = np.zeros((DENS, 128))
    for t in range(4):
        special[:, 32 * t : 32 * t + 2 * TOP] = doubled[:, 160 * t : 160 * t + 2 * TOP]
    weights = np.zeros((2, COUNT, 256, 256), ml_dtypes.bfloat16)
    for k, offset in enumerate(EVEN_OFFSETS):
        core = np.zeros((512, 512))
        core[np.ix_(main, main)] = (inverse @ kernels[offset] @ inverse.T).T
        leading = core[np.ix_(high, high)]
        core[np.ix_(low, high)] = leading
        core[np.ix_(high, low)] = leading - rounded(leading)
        weights[0, k] = core[:256, :256].astype(ml_dtypes.bfloat16)
        weights[1, k] = core[256:, 256:].astype(ml_dtypes.bfloat16)
    picks = np.zeros((2, 2, len(ALL_OFFSETS), 128), ml_dtypes.bfloat16)
    for cx in range(2):
        for cy in range(2):
            for k, (a, b) in enumerate(EVEN_OFFSETS):
                offset = (-a if cx else a, -b if cy else b)
                picks[cx, cy, ALL_OFFSETS.index(offset), k] = 1
    return {
        "weights": weights.reshape(2, COUNT * 256, 256),
        "doubled": doubled.astype(ml_dtypes.bfloat16),
        "special": special.astype(ml_dtypes.bfloat16),
        "doubled_t": np.ascontiguousarray(doubled.T).astype(ml_dtypes.bfloat16),
        "special_t": np.ascontiguousarray(special.T).astype(ml_dtypes.bfloat16),
        "sign_y": np.tile(sign_y[None, :], (8, 1)).astype(np.float32),
        "picks": picks,
    }


def split(value):
    high = value.astype(BF16)
    return high, (value - high.astype(F32)).astype(BF16)


def mm(a, b):
    return jnp.dot(a, b, preferred_element_type=F32)


def mm_t(a, b):
    return lax.dot_general(a, b, (((1,), (1,)), ((), ())), preferred_element_type=F32)


def product(rows, high_matrix, low_matrix):
    count = rows.shape[0]
    high, low = split(rows)
    both = mm_t(jnp.concatenate([high, low], axis=0), high_matrix)
    return both[:count] + both[count:] + mm_t(high, low_matrix)


def lanes(t):
    return slice(128 * t, 128 * t + 128)


def lane_index(shape):
    return lax.broadcasted_iota(jnp.int32, shape, len(shape) - 1)


def project(rows, doubled, special):
    high, low = split(rows)
    main = mm(high, doubled)
    fine = mm(low, special)
    place = lane_index(fine.shape)
    tiles = []
    for t in range(4):
        tile = main[:, lanes(t)]
        tile = jnp.where((place >= 32 * t) & (place < 32 * t + 32), tile + fine, tile)
        left_over = tile - tile.astype(BF16).astype(F32)
        tiles.append(jnp.where((place >= 32 * t + TOP) & (place < 32 * t + 2 * TOP), left_over, tile))
    return jnp.concatenate(tiles, axis=1)


def expand(y, doubled_t, special_t):
    high = y.astype(BF16)
    rest = y - high.astype(F32)
    place = lane_index((y.shape[0], 128))
    fine = jnp.zeros((y.shape[0], 128), F32)
    for t in range(4):
        fine = jnp.where((place >= 32 * t) & (place < 32 * t + 32), rest[:, lanes(t)], fine)
    return mm(high, doubled_t) + mm(fine.astype(BF16), special_t)


def turned(shape):
    return jnp.where(lax.rem(lax.div(lane_index(shape), 128), 2) == 1, -1.0, 1.0)


DIRECTIONS = [(-1, 0), (1, 0), (0, -1), (0, 1), (-1, -1), (-1, 1), (1, -1), (1, 1)]


def pack_sides(row_of, strips, corners, rows, width):
    half = rows // 2
    for side in range(2):
        for col in range(2):
            y = (width - 2 if side else 0) + col
            for parity in range(2):
                for i in range(half):
                    at = parity * half + i
                    strips[side, col, at : at + 1, :] = row_of(2 * i + parity, y)
    corners[...] = jnp.zeros_like(corners)
    for sx in range(2):
        for sy in range(2):
            for col in range(2):
                y = (width - 2 if sy else 0) + col
                for parity in range(2):
                    x = (rows - 2 if sx else 0) + parity
                    at = 2 * col + parity
                    corners[sx, sy, at : at + 1, :] = row_of(x, y)


def side_copies(block, strips, corners, got_x, got_y, got_c, send, recv, rows, ids):
    copies = []
    for n, (dx, dy) in enumerate(DIRECTIONS):
        sx, sy = (dx + 1) // 2, (dy + 1) // 2
        if dy == 0:
            source = block.at[rows - 2 : rows] if dx > 0 else block.at[0:2]
            target = got_x.at[1 - sx]
        elif dx == 0:
            source, target = strips.at[sy], got_y.at[1 - sy]
        else:
            source, target = corners.at[sx, sy], got_c.at[1 - sx, 1 - sy]
        copies.append(
            pltpu.make_async_remote_copy(
                src_ref=source,
                dst_ref=target,
                send_sem=send.at[n],
                recv_sem=recv.at[n],
                device_id=ids[n],
                device_id_type=MESH,
            )
        )
    return copies


def hold_sides(held, got_y, got_c, doubled, special, strip):
    held[0 : 4 * strip, :] = project(got_y[...].reshape(4 * strip, DENS), doubled, special)
    held[4 * strip : 4 * strip + 32, :] = project(got_c[...].reshape(32, DENS), doubled, special)


def place_sides(put, held, half, strip):
    for side in range(2):
        for col in range(2):
            for parity in range(2):
                for i in range(half):
                    at = (side * 2 + col) * strip + parity * half + i
                    put(parity, 1 + i, side, col, held[at : at + 1, :])
                for sx in range(2):
                    at = 4 * strip + (sx * 2 + side) * 8 + 2 * col + parity
                    put(parity, (half + 1) * sx, side, col, held[at : at + 1, :])


def fill_leaf(padded, children, doubled, special, rows, chunk):
    half = rows // 2
    places = children.shape[2]
    for c in range(0, half, chunk):
        value = children[2 * c : 2 * c + 2 * chunk].reshape(4 * chunk * places, DENS)
        value = project(value, doubled, special).reshape(chunk, 2, 2, places, 512)
        for parity in range(2):
            padded[parity, 1 + c : 1 + c + chunk, :, 8 : 8 + places, :] = value[:, parity]


def fill_leaf_sides(padded, got_x, got_y, got_c, held, doubled, special, rows, places, strip):
    half = rows // 2
    value = project(got_x[...].reshape(8 * places, DENS), doubled, special).reshape(2, 2, 2, places, 512)
    for side in range(2):
        for parity in range(2):
            padded[parity, (half + 1) * side, :, 8 : 8 + places, :] = value[side, parity]
    hold_sides(held, got_y, got_c, doubled, special, strip)

    def put(parity, x, side, col, row):
        y = 8 + places if side else 7
        padded[parity, x, col, y : y + 1, :] = row

    place_sides(put, held, half, strip)


def shift_leaf(padded, shifted, sign_y, places):
    signs = sign_y[0:1, :].reshape(1, 1, 512)
    for d in range(6):
        step = d - 2
        for parity in range(2):
            found = []
            for target in range(2):
                source = target + (-step if target else step)
                start = 8 + source // 2
                value = padded[parity, :, source % 2, start : start + places, :]
                found.append(value * signs if target else value)
            shifted[d, parity] = jnp.concatenate(found, axis=1).astype(BF16)


def fill_parent(padded, block, doubled, special, rows, width):
    half = rows // 2
    value = project(block[...].reshape(rows * width, DENS), doubled, special).reshape(half, 2, width, 512)
    for parity in range(2):
        padded[parity, 1 : 1 + half, 8 : 8 + width, :] = value[:, parity]
    zero = jnp.zeros((half + 2, 8, 512), F32)
    for parity in range(2):
        padded[parity, :, 0:8, :] = zero
        padded[parity, :, 8 + width : 16 + width, :] = zero


def fill_parent_sides(padded, got_x, got_y, got_c, held, doubled, special, rows, width, strip):
    half = rows // 2
    value = project(got_x[...].reshape(4 * width, DENS), doubled, special).reshape(2, 2, width, 512)
    for side in range(2):
        for parity in range(2):
            padded[parity, (half + 1) * side, 8 : 8 + width, :] = value[side, parity]
    hold_sides(held, got_y, got_c, doubled, special, strip)

    def put(parity, x, side, col, row):
        y = 8 + width + col if side else 6 + col
        padded[parity, x, y : y + 1, :] = row

    place_sides(put, held, half, strip)


def shift_parent(padded, shifted, sign_y, width):
    row = lax.broadcasted_iota(jnp.int32, (padded.shape[1], width, 512), 1)
    even = lax.rem(row, 2) == 0
    signs = sign_y[0:1, :].reshape(1, 1, 512)
    for d in range(6):
        step = d - 2
        for parity in range(2):
            forward = padded[parity, :, 8 + step : 8 + step + width, :]
            backward = padded[parity, :, 8 - step : 8 - step + width, :] * signs
            shifted[d, parity] = jnp.where(even, forward, backward)


def leaf_flags(lists, picks, rows, width):
    half, places = rows // 2, width // 2
    block = lists[...].astype(F32).reshape(half, 2, places, 2, len(ALL_OFFSETS))
    found = []
    for cx in range(2):
        pair = []
        for cy in range(2):
            part = block[:, cx, :, cy, :].reshape(half * places, len(ALL_OFFSETS)).astype(BF16)
            pair.append(mm(part, picks[cx, cy]).reshape(half, places, 128))
        found.append(jnp.concatenate(pair, axis=1))
    return found


def parent_flags(lists, picks, rows, width):
    half = rows // 2
    block = lists[...].astype(F32).reshape(half, 2, width, len(ALL_OFFSETS))
    even = lax.rem(lax.broadcasted_iota(jnp.int32, (half, width, 128), 1), 2) == 0
    found = []
    for cx in range(2):
        part = block[:, cx].reshape(half * width, len(ALL_OFFSETS)).astype(BF16)
        pair = [mm(part, picks[cx, cy]).reshape(half, width, 128) for cy in range(2)]
        found.append(jnp.where(even, pair[0], pair[1]))
    return found


def interact(levels, weights, total, group):
    for first in range(0, COUNT, group):
        last = min(first + group, COUNT)
        parts = [[], []]
        for k in range(first, last):
            a, b = EVEN_OFFSETS[k]
            pieces = [[] for _ in range(4)]
            for shifted, flags, half, width in levels:
                for cx in range(2):
                    source = cx + (-a if cx else a)
                    parity, start = source % 2, source // 2 + 1
                    flag = flags[cx, :, :, k : k + 1]
                    flag = jnp.broadcast_to(flag, (half, width, 128)).astype(shifted.dtype)
                    for t in range(4):
                        mask = -flag if (cx and t % 2) else flag
                        piece = shifted[b + 2, parity, start : start + half, :, lanes(t)] * mask
                        pieces[t].append(piece.reshape(half * width, 128).astype(BF16))
            for t in range(4):
                parts[t // 2].append(jnp.concatenate(pieces[t], axis=0))
        for z in range(2):
            term = mm(jnp.concatenate(parts[z], axis=1), weights[z, first * 256 : last * 256, :])
            cols = slice(256 * z, 256 * z + 256)
            if first == 0:
                total[:, cols] = term
            else:
                total[:, cols] += term


def near_body(
    sizes,
    leaf_hbm, parent_in_hbm, leaf_lists_hbm, parent_lists_hbm, up_hbm, down_hbm, inverse_hbm,
    weights_hbm, doubled_hbm, special_hbm, doubled_t_hbm, special_t_hbm, sign_hbm, picks_hbm,
    leaf_check, parent_up,
    leaf, parent_in, leaf_lists, parent_lists, up, down, inverse,
    weights, doubled, special, doubled_t, special_t, sign_y, picks,
    down_high, down_low, inverse_high, inverse_low,
    leaf_strips, leaf_corners, leaf_got_x, leaf_got_y, leaf_got_c, leaf_held,
    parent_strips, parent_corners, parent_got_x, parent_got_y, parent_got_c, parent_held,
    children, leaf_padded, leaf_shifted, leaf_marks,
    parent_padded, parent_shifted, parent_marks, parent_local, total,
    load_sem, leaf_send, leaf_recv, parent_send, parent_recv,
):
    rows, width, prows, pwidth, gx_size, gy_size = sizes
    half, phalf = rows // 2, prows // 2
    places = width // 2
    gx, gy = lax.axis_index("gx"), lax.axis_index("gy")
    ids = [
        (lax.rem(gx + dx + gx_size, gx_size), lax.rem(gy + dy + gy_size, gy_size)) for dx, dy in DIRECTIONS
    ]
    barrier = pltpu.get_barrier_semaphore()
    for place in ids:
        pl.semaphore_signal(barrier, inc=1, device_id=place, device_id_type=MESH)

    pairs = [(leaf_hbm, leaf)]
    pairs += [(up_hbm.at[c], up.at[c]) for c in range(4)]
    pairs += [(doubled_hbm, doubled), (special_hbm, special), (sign_hbm, sign_y), (picks_hbm, picks)]
    pairs += [(leaf_lists_hbm, leaf_lists), (parent_lists_hbm, parent_lists)]
    pairs += [(down_hbm, down), (inverse_hbm, inverse), (weights_hbm, weights)]
    pairs += [(doubled_t_hbm, doubled_t), (special_t_hbm, special_t), (parent_in_hbm, parent_in)]
    loads = [pltpu.make_async_copy(a, b, load_sem.at[n]) for n, (a, b) in enumerate(pairs)]
    for load in loads:
        load.start()

    loads[0].wait()
    for cy in range(2):
        children[:, cy] = leaf[...].reshape(rows, places, 2, DENS)[:, :, cy, :]
    pack_sides(lambda x, y: leaf[x, y : y + 1, :], leaf_strips, leaf_corners, rows, width)
    for c in range(4):
        loads[1 + c].wait()
        child = children[...].reshape(prows, 2, 2, pwidth, DENS)[:, c // 2, c % 2].reshape(prows * pwidth, DENS)
        term = product(child, *split(up[c])).reshape(prows, pwidth, DENS)
        if c == 0:
            parent_up[...] = term
        else:
            parent_up[...] += term
    pack_sides(lambda x, y: parent_up[x, y : y + 1, :], parent_strips, parent_corners, prows, pwidth)
    pl.semaphore_wait(barrier, len(DIRECTIONS))
    leaf_copies = side_copies(
        children, leaf_strips, leaf_corners, leaf_got_x, leaf_got_y, leaf_got_c, leaf_send, leaf_recv, rows, ids
    )
    parent_copies = side_copies(
        parent_up, parent_strips, parent_corners, parent_got_x, parent_got_y, parent_got_c,
        parent_send, parent_recv, prows, ids,
    )
    for copy in leaf_copies + parent_copies:
        copy.start()

    for load in loads[5:13]:
        load.wait()
    basis = (doubled[...], special[...])
    fill_leaf(leaf_padded, children, *basis, rows, 3)
    fill_parent(parent_padded, parent_up, *basis, prows, pwidth)
    for cx, value in enumerate(leaf_flags(leaf_lists, picks, rows, width)):
        leaf_marks[cx] = value
    for cx, value in enumerate(parent_flags(parent_lists, picks, prows, pwidth)):
        parent_marks[cx] = value
    for c in range(4):
        down_high[c], down_low[c] = split(down[c])
    inverse_high[...], inverse_low[...] = split(inverse[...])
    for load in loads[13:]:
        load.wait()
    for copy in leaf_copies:
        copy.wait()
    fill_leaf_sides(leaf_padded, leaf_got_x, leaf_got_y, leaf_got_c, leaf_held, *basis, rows, places, rows)
    shift_leaf(leaf_padded, leaf_shifted, sign_y, places)
    for copy in parent_copies:
        copy.wait()
    fill_parent_sides(
        parent_padded, parent_got_x, parent_got_y, parent_got_c, parent_held, *basis, prows, pwidth, 16
    )
    shift_parent(parent_padded, parent_shifted, sign_y, pwidth)
    levels = [(leaf_shifted, leaf_marks, half, width), (parent_shifted, parent_marks, phalf, pwidth)]
    interact(levels, weights, total, 3)

    signs = sign_y[0:1, :].reshape(1, 1, 512)
    leaf_count, parent_count = rows * width, prows * pwidth
    y = total[leaf_count : leaf_count + parent_count, :].reshape(2, phalf, pwidth, 512)
    row = lax.broadcasted_iota(jnp.int32, (phalf, pwidth, 512), 1)
    y = [jnp.where(lax.rem(row, 2) == 0, part, part * signs) for part in (y[0], y[1] * turned((1, 1, 512)))]
    y = jnp.concatenate(y, axis=0).reshape(parent_count, 512)
    value = product(expand(y, doubled_t[...], special_t[...]), inverse_high[...], inverse_low[...])
    value = value.reshape(2, phalf, pwidth, DENS)
    for cx in range(2):
        for i in range(phalf):
            parent_local[2 * i + cx] = value[cx, i] + parent_in[2 * i + cx]

    quarter = leaf_count // 4
    for c in range(4):
        y = total[c * quarter : (c + 1) * quarter, :].reshape(half // 2, 2, places, 512)
        if c >= 2:
            y = y * turned((1, 1, 1, 512))
        y = jnp.concatenate([y[:, 0:1], y[:, 1:2] * signs.reshape(1, 1, 1, 512)], axis=1).reshape(quarter, 512)
        value = expand(y, doubled_t[...], special_t[...]).reshape(half // 2, 2, places, DENS)
        for i in range(half // 2):
            leaf_check[2 * (i + (c % 2) * (half // 2)) + c // 2] = value[i]

    local = parent_local[...].reshape(parent_count, DENS)
    for c in range(4):
        value = product(local, down_high[c], down_low[c]).reshape(prows, pwidth, DENS)
        for i in range(prows):
            leaf_check[2 * i + c // 2, c % 2] += value[i]


def last_body(check, parent_up, inverse, leaf_down, parent_out):
    rows, _, places, _ = check.shape
    parent_out[...] = parent_up[...]
    value = product(check[...].reshape(rows * 2 * places, DENS), *split(inverse[...]))
    value = value.reshape(rows, 2, places, DENS)
    pair = [value[:, cy].reshape(rows, places, 1, DENS) for cy in range(2)]
    leaf_down[...] = jnp.concatenate(pair, axis=2).reshape(rows, 2 * places, DENS)


def local(sizes, leaf_up, parent_in, leaf_lists, parent_lists, up_transfer, down_transfer, check_inverse):
    rows, width, prows, pwidth = sizes[:4]
    half, phalf = rows // 2, prows // 2
    places = width // 2
    names = ("weights", "doubled", "special", "doubled_t", "special_t", "sign_y", "picks")
    constants = [jnp.asarray(tables()[name]) for name in names]
    operands = [leaf_up, parent_in, leaf_lists, parent_lists, up_transfer, down_transfer, check_inverse] + constants
    scratch = [pltpu.VMEM(x.shape, x.dtype) for x in operands]
    scratch += [pltpu.VMEM((4, DENS, DENS), BF16)] * 2 + [pltpu.VMEM((DENS, DENS), BF16)] * 2

    def sides(x_shape, strip):
        return [
            pltpu.VMEM((2, 2, strip, DENS), F32),
            pltpu.VMEM((2, 2, 8, DENS), F32),
            pltpu.VMEM((2, 2) + x_shape + (DENS,), F32),
            pltpu.VMEM((2, 2, strip, DENS), F32),
            pltpu.VMEM((2, 2, 8, DENS), F32),
            pltpu.VMEM((4 * strip + 32, 512), F32),
        ]

    scratch += sides((2, places), rows) + sides((pwidth,), 16)
    scratch += [
        pltpu.VMEM((rows, 2, places, DENS), F32),
        pltpu.VMEM((2, half + 2, 2, 16 + places, 512), F32),
        pltpu.VMEM((6, 2, half + 2, width, 512), BF16),
        pltpu.VMEM((2, half, width, 128), F32),
        pltpu.VMEM((2, phalf + 2, 16 + pwidth, 512), F32),
        pltpu.VMEM((6, 2, phalf + 2, pwidth, 512), F32),
        pltpu.VMEM((2, phalf, pwidth, 128), F32),
        pltpu.VMEM((prows, pwidth, DENS), F32),
        pltpu.VMEM((rows * width + prows * pwidth, 512), F32),
        pltpu.SemaphoreType.DMA((17,)),
        pltpu.SemaphoreType.DMA((8,)),
        pltpu.SemaphoreType.DMA((8,)),
        pltpu.SemaphoreType.DMA((8,)),
        pltpu.SemaphoreType.DMA((8,)),
    ]
    check, parent_up = pl.pallas_call(
        functools.partial(near_body, sizes),
        out_shape=(
            pltpu.VMEM((rows, 2, places, DENS), F32),
            pltpu.VMEM((prows, pwidth, DENS), F32),
        ),
        in_specs=[pl.BlockSpec(memory_space=pltpu.HBM)] * len(operands),
        out_specs=(pl.BlockSpec(memory_space=pltpu.VMEM),) * 2,
        scratch_shapes=scratch,
        compiler_params=pltpu.CompilerParams(
            collective_id=0, has_side_effects=True, vmem_limit_bytes=60 * 1024 * 1024
        ),
    )(*operands)
    return pl.pallas_call(
        last_body,
        out_shape=(
            jax.ShapeDtypeStruct((rows, width, DENS), F32),
            jax.ShapeDtypeStruct((prows, pwidth, DENS), F32),
        ),
        in_specs=[pl.BlockSpec(memory_space=pltpu.VMEM)] * 3,
        out_specs=(pl.BlockSpec(memory_space=pltpu.VMEM),) * 2,
        compiler_params=pltpu.CompilerParams(vmem_limit_bytes=16 * 1024 * 1024),
    )(check, parent_up, check_inverse)


def solution(mesh):
    gx_size, gy_size = mesh.shape["gx"], mesh.shape["gy"]
    sizes = (192 // gx_size, 256 // gy_size, 96 // gx_size, 128 // gy_size, gx_size, gy_size)
    placed = (P("gx", "gy", None),) * 4 + (P(), P(), P())
    return jax.shard_map(
        functools.partial(local, sizes),
        mesh=mesh,
        in_specs=placed,
        out_specs=(P("gx", "gy", None), P("gx", "gy", None)),
        check_vma=False,
    )
```

```python
import functools
import itertools

import jax
import jax.numpy as jnp
import ml_dtypes
import numpy as np
from jax import lax
from jax.experimental import pallas as pl
from jax.experimental.pallas import tpu as pltpu
from jax.sharding import PartitionSpec as P

ORDER = 6
DENS = 456
TOP = 14
F32 = jnp.float32
BF16 = jnp.bfloat16
MESH = pl.DeviceIdType.MESH

ALL_OFFSETS = [(a, b) for a in range(-3, 4) for b in range(-3, 4) if max(abs(a), abs(b)) >= 2]
EVEN_OFFSETS = [(a, b) for a in range(-2, 4) for b in range(-2, 4) if max(abs(a), abs(b)) >= 2]
COUNT = len(EVEN_OFFSETS)


def rounded(values):
    return values.astype(ml_dtypes.bfloat16).astype(np.float64)


def surface_points():
    grid_line = np.linspace(-1.0, 1.0, ORDER)
    points = []
    for i in range(ORDER):
        for j in range(ORDER):
            for k in range(ORDER):
                if min(i, j, k) == 0 or max(i, j, k) == ORDER - 1:
                    points.append((grid_line[i], grid_line[j], grid_line[k]))
    return np.array(points)


def kernel_matrix(points, shift):
    r = 0.525 * (points[:, None, :] - points[None, :, :]) - np.array([shift[0], shift[1], 0.0])
    length = np.sqrt((r * r).sum(-1))
    count = len(points)
    matrix = np.zeros((3, count, 3, count))
    for a in range(3):
        for b in range(3):
            matrix[a, :, b, :] = (float(a == b) / length + r[..., a] * r[..., b] / length**3) / (8.0 * np.pi)
    return matrix.reshape(3 * count, 3 * count)


def mirror_basis(points, signs):
    count = len(points)
    place = {tuple(np.round(p * (ORDER - 1)).astype(int)): i for i, p in enumerate(points)}
    corner = [i for i, p in enumerate(points) if (p > 0).all()]
    basis = np.zeros((3 * count, 3 * len(corner)))
    for a in range(3):
        for h, i in enumerate(corner):
            for flip in itertools.product([1, -1], repeat=3):
                j = place[tuple(np.round(points[i] * np.array(flip) * (ORDER - 1)).astype(int))]
                sign = 1
                for axis in range(3):
                    if flip[axis] == -1:
                        sign *= signs[axis] * (-1 if axis == a else 1)
                basis[a * count + j, a * len(corner) + h] = sign
    return basis / np.sqrt(8.0)


@functools.lru_cache(maxsize=1)
def tables():
    points = surface_points()
    kernels = {o: kernel_matrix(points, o) for o in ALL_OFFSETS}
    stacked = np.concatenate([kernels[o] for o in ALL_OFFSETS], axis=1)
    basis = np.zeros((DENS, 512))
    sign_y = np.ones(512)
    high, low, main = [], [], []
    for t, (sx, sz) in enumerate([(1, 1), (-1, 1), (1, -1), (-1, -1)]):
        found = []
        for sy in (1, -1):
            mirror = mirror_basis(points, (sx, sy, sz))
            left, size, _ = np.linalg.svd(mirror.T @ stacked, full_matrices=False)
            for j in range(left.shape[1]):
                found.append((size[j], sy, rounded(mirror @ left[:, j])))
        found.sort(key=lambda item: -item[0])
        start = 128 * t + 32 * t
        special = range(start, start + 2 * TOP)
        rest = [lane for lane in range(128 * t, 128 * t + 128) if lane not in special]
        for j, (_, sy, column) in enumerate(found):
            lane = start + j if j < TOP else rest[j - TOP]
            basis[:, lane] = column
            sign_y[lane] = sy
            main.append(lane)
            if j < TOP:
                high.append(lane)
                low.append(lane + TOP)
                sign_y[lane + TOP] = sy
    inverse = np.linalg.inv(basis[:, main])
    doubled = basis.copy()
    doubled[:, low] = basis[:, high]
    special = np.zeros((DENS, 128))
    for t in range(4):
        special[:, 32 * t : 32 * t + 2 * TOP] = doubled[:, 160 * t : 160 * t + 2 * TOP]
    weights = np.zeros((2, COUNT, 256, 256), ml_dtypes.bfloat16)
    for k, offset in enumerate(EVEN_OFFSETS):
        core = np.zeros((512, 512))
        core[np.ix_(main, main)] = (inverse @ kernels[offset] @ inverse.T).T
        leading = core[np.ix_(high, high)]
        core[np.ix_(low, high)] = leading
        core[np.ix_(high, low)] = leading - rounded(leading)
        weights[0, k] = core[:256, :256].astype(ml_dtypes.bfloat16)
        weights[1, k] = core[256:, 256:].astype(ml_dtypes.bfloat16)
    picks = np.zeros((2, 2, len(ALL_OFFSETS), 128), ml_dtypes.bfloat16)
    for cx in range(2):
        for cy in range(2):
            for k, (a, b) in enumerate(EVEN_OFFSETS):
                offset = (-a if cx else a, -b if cy else b)
                picks[cx, cy, ALL_OFFSETS.index(offset), k] = 1
    return {
        "weights": weights.reshape(2, COUNT * 256, 256),
        "doubled": doubled.astype(ml_dtypes.bfloat16),
        "special": special.astype(ml_dtypes.bfloat16),
        "doubled_t": np.ascontiguousarray(doubled.T).astype(ml_dtypes.bfloat16),
        "special_t": np.ascontiguousarray(special.T).astype(ml_dtypes.bfloat16),
        "sign_y": np.tile(sign_y[None, :], (8, 1)).astype(np.float32),
        "picks": picks,
    }


def split(value):
    high = value.astype(BF16)
    return high, (value - high.astype(F32)).astype(BF16)


def mm(a, b):
    return jnp.dot(a, b, preferred_element_type=F32)


def mm_t(a, b):
    return lax.dot_general(a, b, (((1,), (1,)), ((), ())), preferred_element_type=F32)


def product(rows, high_matrix, low_matrix):
    count = rows.shape[0]
    high, low = split(rows)
    both = mm_t(jnp.concatenate([high, low], axis=0), high_matrix)
    return both[:count] + both[count:] + mm_t(high, low_matrix)


def lanes(t):
    return slice(128 * t, 128 * t + 128)


def lane_index(shape):
    return lax.broadcasted_iota(jnp.int32, shape, len(shape) - 1)


def project(rows, doubled, special):
    high, low = split(rows)
    main = mm(high, doubled)
    fine = mm(low, special)
    place = lane_index(fine.shape)
    tiles = []
    for t in range(4):
        tile = main[:, lanes(t)]
        tile = jnp.where((place >= 32 * t) & (place < 32 * t + 32), tile + fine, tile)
        left_over = tile - tile.astype(BF16).astype(F32)
        tiles.append(jnp.where((place >= 32 * t + TOP) & (place < 32 * t + 2 * TOP), left_over, tile))
    return jnp.concatenate(tiles, axis=1)


def expand(y, doubled_t, special_t):
    high = y.astype(BF16)
    rest = y - high.astype(F32)
    place = lane_index((y.shape[0], 128))
    fine = jnp.zeros((y.shape[0], 128), F32)
    for t in range(4):
        fine = jnp.where((place >= 32 * t) & (place < 32 * t + 32), rest[:, lanes(t)], fine)
    return mm(high, doubled_t) + mm(fine.astype(BF16), special_t)


def turned(shape):
    return jnp.where(lax.rem(lax.div(lane_index(shape), 128), 2) == 1, -1.0, 1.0)


DIRECTIONS = [(-1, 0), (1, 0), (0, -1), (0, 1), (-1, -1), (-1, 1), (1, -1), (1, 1)]


def pack_sides(row_of, strips, corners, rows, width):
    half = rows // 2
    for side in range(2):
        for col in range(2):
            y = (width - 2 if side else 0) + col
            for parity in range(2):
                for i in range(half):
                    at = col * rows + parity * half + i
                    strips[side, at : at + 1, :] = row_of(2 * i + parity, y)
    for sx in range(2):
        for sy in range(2):
            for col in range(2):
                y = (width - 2 if sy else 0) + col
                for parity in range(2):
                    x = (rows - 2 if sx else 0) + parity
                    at = 2 * col + parity
                    corners[sx, sy, at : at + 1, :] = row_of(x, y)


def side_copies(block, strips, corners, got_x, got_y, got_c, send, recv, rows, ids):
    copies = []
    for n, (dx, dy) in enumerate(DIRECTIONS):
        sx, sy = (dx + 1) // 2, (dy + 1) // 2
        if dy == 0:
            source = block.at[rows - 2 : rows] if dx > 0 else block.at[0:2]
            target = got_x.at[1 - sx]
        elif dx == 0:
            source, target = strips.at[sy], got_y.at[1 - sy]
        else:
            source, target = corners.at[sx, sy], got_c.at[1 - sx, 1 - sy]
        copies.append(
            pltpu.make_async_remote_copy(
                src_ref=source,
                dst_ref=target,
                send_sem=send.at[n],
                recv_sem=recv.at[n],
                device_id=ids[n],
                device_id_type=MESH,
            )
        )
    return copies


def project_sides(held, got_x, got_y, got_c, doubled, special):
    parts = [got_x[...].reshape(-1, DENS), got_y[...].reshape(-1, DENS)]
    parts += [got_c[sx, sy] for sx in range(2) for sy in range(2)]
    held[...] = project(jnp.concatenate(parts, axis=0), doubled, special)


def place_sides(put, held, first, rows):
    half = rows // 2
    for side in range(2):
        for col in range(2):
            for parity in range(2):
                for i in range(half):
                    at = first + (side * 2 + col) * rows + parity * half + i
                    put(parity, 1 + i, side, col, held[at : at + 1, :])
                for sx in range(2):
                    at = first + 4 * rows + (sx * 2 + side) * 4 + 2 * col + parity
                    put(parity, (half + 1) * sx, side, col, held[at : at + 1, :])


def fill_leaf(padded, children, doubled, special, rows, chunk):
    half = rows // 2
    places = children.shape[2]
    for c in range(0, half, chunk):
        value = children[2 * c : 2 * c + 2 * chunk].reshape(4 * chunk * places, DENS)
        value = project(value, doubled, special).reshape(chunk, 2, 2, places, 512)
        for parity in range(2):
            padded[parity, 1 + c : 1 + c + chunk, :, 8 : 8 + places, :] = value[:, parity]


def fill_leaf_sides(padded, held, rows, places):
    half = rows // 2
    value = held[0 : 8 * places, :].reshape(2, 2, 2, places, 512)
    for side in range(2):
        for parity in range(2):
            padded[parity, (half + 1) * side, :, 8 : 8 + places, :] = value[side, parity]

    def put(parity, x, side, col, row):
        y = 8 + places if side else 7
        padded[parity, x, col, y : y + 1, :] = row

    place_sides(put, held, 8 * places, rows)


def shift_leaf(padded, shifted, sign_y, places):
    signs = sign_y[0:1, :].reshape(1, 1, 512)
    for d in range(6):
        step = d - 2
        for parity in range(2):
            found = []
            for target in range(2):
                source = target + (-step if target else step)
                start = 8 + source // 2
                value = padded[parity, :, source % 2, start : start + places, :]
                found.append(value * signs if target else value)
            shifted[d, parity] = jnp.concatenate(found, axis=1).astype(BF16)


def fill_parent(padded, block, doubled, special, rows, width):
    half = rows // 2
    value = project(block[...].reshape(rows * width, DENS), doubled, special).reshape(half, 2, width, 512)
    for parity in range(2):
        padded[parity, 1 : 1 + half, 8 : 8 + width, :] = value[:, parity]
    zero = jnp.zeros((half + 2, 8, 512), F32)
    for parity in range(2):
        padded[parity, :, 0:8, :] = zero
        padded[parity, :, 8 + width : 16 + width, :] = zero


def fill_parent_sides(padded, held, rows, width):
    half = rows // 2
    value = held[0 : 4 * width, :].reshape(2, 2, width, 512)
    for side in range(2):
        for parity in range(2):
            padded[parity, (half + 1) * side, 8 : 8 + width, :] = value[side, parity]

    def put(parity, x, side, col, row):
        y = 8 + width + col if side else 6 + col
        padded[parity, x, y : y + 1, :] = row

    place_sides(put, held, 4 * width, rows)


def shift_parent(padded, shifted, sign_y, width):
    row = lax.broadcasted_iota(jnp.int32, (padded.shape[1], width, 512), 1)
    even = lax.rem(row, 2) == 0
    signs = sign_y[0:1, :].reshape(1, 1, 512)
    for d in range(6):
        step = d - 2
        for parity in range(2):
            forward = padded[parity, :, 8 + step : 8 + step + width, :]
            backward = padded[parity, :, 8 - step : 8 - step + width, :] * signs
            shifted[d, parity] = jnp.where(even, forward, backward)


def leaf_flags(lists, picks, rows, width):
    half, places = rows // 2, width // 2
    block = lists[...].astype(F32).reshape(half, 2, places, 2, len(ALL_OFFSETS))
    found = []
    for cx in range(2):
        pair = []
        for cy in range(2):
            part = block[:, cx, :, cy, :].reshape(half * places, len(ALL_OFFSETS)).astype(BF16)
            pair.append(mm(part, picks[cx, cy]).reshape(half, places, 128))
        found.append(jnp.concatenate(pair, axis=1))
    return found


def parent_flags(lists, picks, rows, width):
    half = rows // 2
    block = lists[...].astype(F32).reshape(half, 2, width, len(ALL_OFFSETS))
    even = lax.rem(lax.broadcasted_iota(jnp.int32, (half, width, 128), 1), 2) == 0
    found = []
    for cx in range(2):
        part = block[:, cx].reshape(half * width, len(ALL_OFFSETS)).astype(BF16)
        pair = [mm(part, picks[cx, cy]).reshape(half, width, 128) for cy in range(2)]
        found.append(jnp.where(even, pair[0], pair[1]))
    return found


def interact(levels, weights, total, group):
    for first in range(0, COUNT, group):
        last = min(first + group, COUNT)
        parts = [[], []]
        for k in range(first, last):
            a, b = EVEN_OFFSETS[k]
            pieces = [[] for _ in range(4)]
            for shifted, flags, half, width in levels:
                for cx in range(2):
                    source = cx + (-a if cx else a)
                    parity, start = source % 2, source // 2 + 1
                    flag = flags[cx, :, :, k : k + 1]
                    flag = jnp.broadcast_to(flag, (half, width, 128)).astype(shifted.dtype)
                    for t in range(4):
                        mask = -flag if (cx and t % 2) else flag
                        piece = shifted[b + 2, parity, start : start + half, :, lanes(t)] * mask
                        pieces[t].append(piece.reshape(half * width, 128).astype(BF16))
            for t in range(4):
                parts[t // 2].append(jnp.concatenate(pieces[t], axis=0))
        for z in range(2):
            term = mm(jnp.concatenate(parts[z], axis=1), weights[z, first * 256 : last * 256, :])
            cols = slice(256 * z, 256 * z + 256)
            if first == 0:
                total[:, cols] = term
            else:
                total[:, cols] += term


def near_body(
    sizes,
    leaf_hbm, parent_in_hbm, leaf_lists_hbm, parent_lists_hbm, up_hbm, down_hbm, inverse_hbm,
    weights_hbm, doubled_hbm, special_hbm, doubled_t_hbm, special_t_hbm, sign_hbm, picks_hbm,
    leaf_check, parent_up, inverse_high, inverse_low,
    leaf, parent_in, leaf_lists, parent_lists, up, down, inverse,
    weights, doubled, special, doubled_t, special_t, sign_y, picks,
    down_high, down_low,
    leaf_strips, leaf_corners, leaf_got_x, leaf_got_y, leaf_got_c, leaf_held,
    parent_strips, parent_corners, parent_got_x, parent_got_y, parent_got_c, parent_held,
    children, leaf_padded, leaf_shifted, leaf_marks,
    parent_padded, parent_shifted, parent_marks, parent_local, total,
    load_sem, leaf_send, leaf_recv, parent_send, parent_recv,
):
    rows, width, prows, pwidth, gx_size, gy_size = sizes
    half, phalf = rows // 2, prows // 2
    places = width // 2
    gx, gy = lax.axis_index("gx"), lax.axis_index("gy")
    ids = [
        (lax.rem(gx + dx + gx_size, gx_size), lax.rem(gy + dy + gy_size, gy_size)) for dx, dy in DIRECTIONS
    ]
    barrier = pltpu.get_barrier_semaphore()
    for place in ids:
        pl.semaphore_signal(barrier, inc=1, device_id=place, device_id_type=MESH)

    pairs = [(leaf_hbm, leaf)]
    pairs += [(up_hbm.at[c], up.at[c]) for c in range(4)]
    pairs += [(doubled_hbm, doubled), (special_hbm, special), (sign_hbm, sign_y), (picks_hbm, picks)]
    pairs += [(leaf_lists_hbm, leaf_lists), (parent_lists_hbm, parent_lists)]
    pairs += [(down_hbm, down), (inverse_hbm, inverse), (weights_hbm, weights)]
    pairs += [(doubled_t_hbm, doubled_t), (special_t_hbm, special_t), (parent_in_hbm, parent_in)]
    loads = [pltpu.make_async_copy(a, b, load_sem.at[n]) for n, (a, b) in enumerate(pairs)]
    for load in loads:
        load.start()

    loads[0].wait()
    for cy in range(2):
        children[:, cy] = leaf[...].reshape(rows, places, 2, DENS)[:, :, cy, :]
    pack_sides(lambda x, y: leaf[x, y : y + 1, :], leaf_strips, leaf_corners, rows, width)
    pl.semaphore_wait(barrier, len(DIRECTIONS))
    leaf_copies = side_copies(
        children, leaf_strips, leaf_corners, leaf_got_x, leaf_got_y, leaf_got_c, leaf_send, leaf_recv, rows, ids
    )
    for copy in leaf_copies:
        copy.start()
    for c in range(4):
        loads[1 + c].wait()
        child = children[...].reshape(prows, 2, 2, pwidth, DENS)[:, c // 2, c % 2].reshape(prows * pwidth, DENS)
        term = product(child, *split(up[c])).reshape(prows, pwidth, DENS)
        if c == 0:
            parent_up[...] = term
        else:
            parent_up[...] += term
    pack_sides(lambda x, y: parent_up[x, y : y + 1, :], parent_strips, parent_corners, prows, pwidth)
    parent_copies = side_copies(
        parent_up, parent_strips, parent_corners, parent_got_x, parent_got_y, parent_got_c,
        parent_send, parent_recv, prows, ids,
    )
    for copy in parent_copies:
        copy.start()

    for load in loads[5:13]:
        load.wait()
    basis = (doubled[...], special[...])
    fill_leaf(leaf_padded, children, *basis, rows, 3)
    fill_parent(parent_padded, parent_up, *basis, prows, pwidth)
    for cx, value in enumerate(leaf_flags(leaf_lists, picks, rows, width)):
        leaf_marks[cx] = value
    for cx, value in enumerate(parent_flags(parent_lists, picks, prows, pwidth)):
        parent_marks[cx] = value
    for c in range(4):
        down_high[c], down_low[c] = split(down[c])
    inverse_high[...], inverse_low[...] = split(inverse[...])
    for load in loads[13:]:
        load.wait()
    for copy in leaf_copies:
        copy.wait()
    project_sides(leaf_held, leaf_got_x, leaf_got_y, leaf_got_c, *basis)
    fill_leaf_sides(leaf_padded, leaf_held, rows, places)
    shift_leaf(leaf_padded, leaf_shifted, sign_y, places)
    for copy in parent_copies:
        copy.wait()
    project_sides(parent_held, parent_got_x, parent_got_y, parent_got_c, *basis)
    fill_parent_sides(parent_padded, parent_held, prows, pwidth)
    shift_parent(parent_padded, parent_shifted, sign_y, pwidth)
    levels = [(leaf_shifted, leaf_marks, half, width), (parent_shifted, parent_marks, phalf, pwidth)]
    interact(levels, weights, total, 3)

    signs = sign_y[0:1, :].reshape(1, 1, 512)
    leaf_count, parent_count = rows * width, prows * pwidth
    y = total[leaf_count : leaf_count + parent_count, :].reshape(2, phalf, pwidth, 512)
    row = lax.broadcasted_iota(jnp.int32, (phalf, pwidth, 512), 1)
    y = [jnp.where(lax.rem(row, 2) == 0, part, part * signs) for part in (y[0], y[1] * turned((1, 1, 512)))]
    y = jnp.concatenate(y, axis=0).reshape(parent_count, 512)
    value = product(expand(y, doubled_t[...], special_t[...]), inverse_high[...], inverse_low[...])
    value = value.reshape(2, phalf, pwidth, DENS)
    for cx in range(2):
        for i in range(phalf):
            parent_local[2 * i + cx] = value[cx, i] + parent_in[2 * i + cx]

    quarter = leaf_count // 4
    for c in range(4):
        y = total[c * quarter : (c + 1) * quarter, :].reshape(half // 2, 2, places, 512)
        if c >= 2:
            y = y * turned((1, 1, 1, 512))
        y = jnp.concatenate([y[:, 0:1], y[:, 1:2] * signs.reshape(1, 1, 1, 512)], axis=1).reshape(quarter, 512)
        value = expand(y, doubled_t[...], special_t[...]).reshape(half // 2, 2, places, DENS)
        for i in range(half // 2):
            leaf_check[2 * (i + (c % 2) * (half // 2)) + c // 2] = value[i]

    local = parent_local[...].reshape(parent_count, DENS)
    for c in range(4):
        value = product(local, down_high[c], down_low[c]).reshape(prows, pwidth, DENS)
        for i in range(prows):
            leaf_check[2 * i + c // 2, c % 2] += value[i]


def last_body(check, parent_up, high, low, leaf_down_hbm, parent_up_hbm, leaf_down, sem):
    rows, _, places, _ = check.shape
    copies = [pltpu.make_async_copy(parent_up, parent_up_hbm, sem.at[0])]
    copies[0].start()
    part = rows // 2
    for c in range(2):
        here = slice(part * c, part * c + part)
        value = product(check[here].reshape(part * 2 * places, DENS), high[...], low[...])
        value = value.reshape(part, 2, places, DENS)
        pair = [value[:, cy].reshape(part, places, 1, DENS) for cy in range(2)]
        leaf_down[here] = jnp.concatenate(pair, axis=2).reshape(part, 2 * places, DENS)
        copies.append(pltpu.make_async_copy(leaf_down.at[here], leaf_down_hbm.at[here], sem.at[1 + c]))
        copies[-1].start()
    for copy in copies:
        copy.wait()


def local(sizes, leaf_up, parent_in, leaf_lists, parent_lists, up_transfer, down_transfer, check_inverse):
    rows, width, prows, pwidth = sizes[:4]
    half, phalf = rows // 2, prows // 2
    places = width // 2
    names = ("weights", "doubled", "special", "doubled_t", "special_t", "sign_y", "picks")
    constants = [jnp.asarray(tables()[name]) for name in names]
    operands = [leaf_up, parent_in, leaf_lists, parent_lists, up_transfer, down_transfer, check_inverse] + constants
    scratch = [pltpu.VMEM(x.shape, x.dtype) for x in operands]
    scratch += [pltpu.VMEM((4, DENS, DENS), BF16)] * 2

    def sides(x_shape, rows_here, total):
        return [
            pltpu.VMEM((2, 2 * rows_here, DENS), F32),
            pltpu.VMEM((2, 2, 4, DENS), F32),
            pltpu.VMEM((2, 2) + x_shape + (DENS,), F32),
            pltpu.VMEM((2, 2 * rows_here, DENS), F32),
            pltpu.VMEM((2, 2, 4, DENS), F32),
            pltpu.VMEM((total, 512), F32),
        ]

    scratch += sides((2, places), rows, 4 * width + 4 * rows + 16)
    scratch += sides((pwidth,), prows, 4 * pwidth + 4 * prows + 16)
    scratch += [
        pltpu.VMEM((rows, 2, places, DENS), F32),
        pltpu.VMEM((2, half + 2, 2, 16 + places, 512), F32),
        pltpu.VMEM((6, 2, half + 2, width, 512), BF16),
        pltpu.VMEM((2, half, width, 128), F32),
        pltpu.VMEM((2, phalf + 2, 16 + pwidth, 512), F32),
        pltpu.VMEM((6, 2, phalf + 2, pwidth, 512), F32),
        pltpu.VMEM((2, phalf, pwidth, 128), F32),
        pltpu.VMEM((prows, pwidth, DENS), F32),
        pltpu.VMEM((rows * width + prows * pwidth, 512), F32),
        pltpu.SemaphoreType.DMA((17,)),
        pltpu.SemaphoreType.DMA((8,)),
        pltpu.SemaphoreType.DMA((8,)),
        pltpu.SemaphoreType.DMA((8,)),
        pltpu.SemaphoreType.DMA((8,)),
    ]
    check, parent_up, high, low = pl.pallas_call(
        functools.partial(near_body, sizes),
        out_shape=(
            pltpu.VMEM((rows, 2, places, DENS), F32),
            pltpu.VMEM((prows, pwidth, DENS), F32),
            pltpu.VMEM((DENS, DENS), BF16),
            pltpu.VMEM((DENS, DENS), BF16),
        ),
        in_specs=[pl.BlockSpec(memory_space=pltpu.HBM)] * len(operands),
        out_specs=(pl.BlockSpec(memory_space=pltpu.VMEM),) * 4,
        scratch_shapes=scratch,
        compiler_params=pltpu.CompilerParams(
            collective_id=0, has_side_effects=True, vmem_limit_bytes=60 * 1024 * 1024
        ),
    )(*operands)
    return pl.pallas_call(
        last_body,
        out_shape=(
            jax.ShapeDtypeStruct((rows, width, DENS), F32),
            jax.ShapeDtypeStruct((prows, pwidth, DENS), F32),
        ),
        in_specs=[pl.BlockSpec(memory_space=pltpu.VMEM)] * 4,
        out_specs=(pl.BlockSpec(memory_space=pltpu.HBM),) * 2,
        scratch_shapes=[pltpu.VMEM((rows, width, DENS), F32), pltpu.SemaphoreType.DMA((3,))],
        compiler_params=pltpu.CompilerParams(vmem_limit_bytes=16 * 1024 * 1024),
    )(check, parent_up, high, low)


def solution(mesh):
    gx_size, gy_size = mesh.shape["gx"], mesh.shape["gy"]
    sizes = (192 // gx_size, 256 // gy_size, 96 // gx_size, 128 // gy_size, gx_size, gy_size)
    placed = (P("gx", "gy", None),) * 4 + (P(), P(), P())
    return jax.shard_map(
        functools.partial(local, sizes),
        mesh=mesh,
        in_specs=placed,
        out_specs=(P("gx", "gy", None), P("gx", "gy", None)),
        check_vma=False,
    )
```

```python
import functools
import itertools

import jax
import jax.numpy as jnp
import ml_dtypes
import numpy as np
from jax import lax
from jax.experimental import pallas as pl
from jax.experimental.pallas import tpu as pltpu
from jax.sharding import PartitionSpec as P

ORDER = 6
DENS = 456
TOP = 14
F32 = jnp.float32
BF16 = jnp.bfloat16
MESH = pl.DeviceIdType.MESH

ALL_OFFSETS = [(a, b) for a in range(-3, 4) for b in range(-3, 4) if max(abs(a), abs(b)) >= 2]
EVEN_OFFSETS = [(a, b) for a in range(-2, 4) for b in range(-2, 4) if max(abs(a), abs(b)) >= 2]
COUNT = len(EVEN_OFFSETS)


def rounded(values):
    return values.astype(ml_dtypes.bfloat16).astype(np.float64)


def surface_points():
    grid_line = np.linspace(-1.0, 1.0, ORDER)
    points = []
    for i in range(ORDER):
        for j in range(ORDER):
            for k in range(ORDER):
                if min(i, j, k) == 0 or max(i, j, k) == ORDER - 1:
                    points.append((grid_line[i], grid_line[j], grid_line[k]))
    return np.array(points)


def kernel_matrix(points, shift):
    r = 0.525 * (points[:, None, :] - points[None, :, :]) - np.array([shift[0], shift[1], 0.0])
    length = np.sqrt((r * r).sum(-1))
    count = len(points)
    matrix = np.zeros((3, count, 3, count))
    for a in range(3):
        for b in range(3):
            matrix[a, :, b, :] = (float(a == b) / length + r[..., a] * r[..., b] / length**3) / (8.0 * np.pi)
    return matrix.reshape(3 * count, 3 * count)


def mirror_basis(points, signs):
    count = len(points)
    place = {tuple(np.round(p * (ORDER - 1)).astype(int)): i for i, p in enumerate(points)}
    corner = [i for i, p in enumerate(points) if (p > 0).all()]
    basis = np.zeros((3 * count, 3 * len(corner)))
    for a in range(3):
        for h, i in enumerate(corner):
            for flip in itertools.product([1, -1], repeat=3):
                j = place[tuple(np.round(points[i] * np.array(flip) * (ORDER - 1)).astype(int))]
                sign = 1
                for axis in range(3):
                    if flip[axis] == -1:
                        sign *= signs[axis] * (-1 if axis == a else 1)
                basis[a * count + j, a * len(corner) + h] = sign
    return basis / np.sqrt(8.0)


@functools.lru_cache(maxsize=1)
def tables():
    points = surface_points()
    kernels = {o: kernel_matrix(points, o) for o in ALL_OFFSETS}
    stacked = np.concatenate([kernels[o] for o in ALL_OFFSETS], axis=1)
    basis = np.zeros((DENS, 512))
    sign_y = np.ones(512)
    high, low, main = [], [], []
    for t, (sx, sz) in enumerate([(1, 1), (-1, 1), (1, -1), (-1, -1)]):
        found = []
        for sy in (1, -1):
            mirror = mirror_basis(points, (sx, sy, sz))
            left, size, _ = np.linalg.svd(mirror.T @ stacked, full_matrices=False)
            for j in range(left.shape[1]):
                found.append((size[j], sy, rounded(mirror @ left[:, j])))
        found.sort(key=lambda item: -item[0])
        start = 128 * t + 32 * t
        special = range(start, start + 2 * TOP)
        rest = [lane for lane in range(128 * t, 128 * t + 128) if lane not in special]
        for j, (_, sy, column) in enumerate(found):
            lane = start + j if j < TOP else rest[j - TOP]
            basis[:, lane] = column
            sign_y[lane] = sy
            main.append(lane)
            if j < TOP:
                high.append(lane)
                low.append(lane + TOP)
                sign_y[lane + TOP] = sy
    inverse = np.linalg.inv(basis[:, main])
    doubled = basis.copy()
    doubled[:, low] = basis[:, high]
    special = np.zeros((DENS, 128))
    for t in range(4):
        special[:, 32 * t : 32 * t + 2 * TOP] = doubled[:, 160 * t : 160 * t + 2 * TOP]
    weights = np.zeros((2, COUNT, 256, 256), ml_dtypes.bfloat16)
    for k, offset in enumerate(EVEN_OFFSETS):
        core = np.zeros((512, 512))
        core[np.ix_(main, main)] = (inverse @ kernels[offset] @ inverse.T).T
        leading = core[np.ix_(high, high)]
        core[np.ix_(low, high)] = leading
        core[np.ix_(high, low)] = leading - rounded(leading)
        weights[0, k] = core[:256, :256].astype(ml_dtypes.bfloat16)
        weights[1, k] = core[256:, 256:].astype(ml_dtypes.bfloat16)
    picks = np.zeros((2, 2, len(ALL_OFFSETS), 128), ml_dtypes.bfloat16)
    for cx in range(2):
        for cy in range(2):
            for k, (a, b) in enumerate(EVEN_OFFSETS):
                offset = (-a if cx else a, -b if cy else b)
                picks[cx, cy, ALL_OFFSETS.index(offset), k] = 1
    return {
        "weights": weights.reshape(2, COUNT * 256, 256),
        "doubled": doubled.astype(ml_dtypes.bfloat16),
        "special": special.astype(ml_dtypes.bfloat16),
        "doubled_t": np.ascontiguousarray(doubled.T).astype(ml_dtypes.bfloat16),
        "special_t": np.ascontiguousarray(special.T).astype(ml_dtypes.bfloat16),
        "sign_y": np.tile(sign_y[None, :], (8, 1)).astype(np.float32),
        "picks": picks,
    }


def split(value):
    high = value.astype(BF16)
    return high, (value - high.astype(F32)).astype(BF16)


def mm(a, b):
    return jnp.dot(a, b, preferred_element_type=F32)


def mm_t(a, b):
    return lax.dot_general(a, b, (((1,), (1,)), ((), ())), preferred_element_type=F32)


def product(rows, high_matrix, low_matrix):
    count = rows.shape[0]
    high, low = split(rows)
    both = mm_t(jnp.concatenate([high, low], axis=0), high_matrix)
    return both[:count] + both[count:] + mm_t(high, low_matrix)


def lanes(t):
    return slice(128 * t, 128 * t + 128)


def lane_index(shape):
    return lax.broadcasted_iota(jnp.int32, shape, len(shape) - 1)


def project(rows, doubled, special):
    high, low = split(rows)
    main = mm(high, doubled)
    fine = mm(low, special)
    place = lane_index(fine.shape)
    tiles = []
    for t in range(4):
        tile = main[:, lanes(t)]
        tile = jnp.where((place >= 32 * t) & (place < 32 * t + 32), tile + fine, tile)
        left_over = tile - tile.astype(BF16).astype(F32)
        tiles.append(jnp.where((place >= 32 * t + TOP) & (place < 32 * t + 2 * TOP), left_over, tile))
    return jnp.concatenate(tiles, axis=1)


def expand(y, doubled_t, special_t):
    high = y.astype(BF16)
    rest = y - high.astype(F32)
    place = lane_index((y.shape[0], 128))
    fine = jnp.zeros((y.shape[0], 128), F32)
    for t in range(4):
        fine = jnp.where((place >= 32 * t) & (place < 32 * t + 32), rest[:, lanes(t)], fine)
    return mm(high, doubled_t) + mm(fine.astype(BF16), special_t)


def turned(shape):
    return jnp.where(lax.rem(lax.div(lane_index(shape), 128), 2) == 1, -1.0, 1.0)


DIRECTIONS = [(0, -1), (0, 1), (-1, -1), (-1, 1), (1, -1), (1, 1), (-1, 0), (1, 0)]


def pack_sides(row_of, strips, corners, rows, width):
    half = rows // 2
    for side in range(2):
        for col in range(2):
            y = (width - 2 if side else 0) + col
            for parity in range(2):
                for i in range(half):
                    at = col * rows + parity * half + i
                    strips[side, at : at + 1, :] = row_of(2 * i + parity, y)
    for sx in range(2):
        for sy in range(2):
            for col in range(2):
                y = (width - 2 if sy else 0) + col
                for parity in range(2):
                    x = (rows - 2 if sx else 0) + parity
                    at = 2 * col + parity
                    corners[sx, sy, at : at + 1, :] = row_of(x, y)


def side_copies(block, strips, corners, got_x, got_y, got_c, send, recv, rows, ids):
    copies = []
    for n, (dx, dy) in enumerate(DIRECTIONS):
        sx, sy = (dx + 1) // 2, (dy + 1) // 2
        if dy == 0:
            source = block.at[rows - 2 : rows] if dx > 0 else block.at[0:2]
            target = got_x.at[1 - sx]
        elif dx == 0:
            source, target = strips.at[sy], got_y.at[1 - sy]
        else:
            source, target = corners.at[sx, sy], got_c.at[1 - sx, 1 - sy]
        copies.append(
            pltpu.make_async_remote_copy(
                src_ref=source,
                dst_ref=target,
                send_sem=send.at[n],
                recv_sem=recv.at[n],
                device_id=ids[n],
                device_id_type=MESH,
            )
        )
    return copies


def finish(copies, n):
    dx, dy = DIRECTIONS[n]
    copies[n].wait_send()
    copies[DIRECTIONS.index((-dx, -dy))].wait_recv()


def project_sides(held, got_x, got_y, got_c, doubled, special):
    parts = [got_x[...].reshape(-1, DENS), got_y[...].reshape(-1, DENS)]
    parts += [got_c[sx, sy] for sx in range(2) for sy in range(2)]
    held[...] = project(jnp.concatenate(parts, axis=0), doubled, special)


def place_sides(put, held, first, rows):
    half = rows // 2
    for side in range(2):
        for col in range(2):
            for parity in range(2):
                for i in range(half):
                    at = first + (side * 2 + col) * rows + parity * half + i
                    put(parity, 1 + i, side, col, held[at : at + 1, :])
                for sx in range(2):
                    at = first + 4 * rows + (sx * 2 + side) * 4 + 2 * col + parity
                    put(parity, (half + 1) * sx, side, col, held[at : at + 1, :])


def fill_leaf(padded, children, doubled, special, rows, chunk):
    half = rows // 2
    places = children.shape[2]
    for c in range(0, half, chunk):
        value = children[2 * c : 2 * c + 2 * chunk].reshape(4 * chunk * places, DENS)
        value = project(value, doubled, special).reshape(chunk, 2, 2, places, 512)
        for parity in range(2):
            padded[parity, 1 + c : 1 + c + chunk, :, 8 : 8 + places, :] = value[:, parity]


def fill_leaf_sides(padded, held, rows, places):
    half = rows // 2
    value = held[0 : 8 * places, :].reshape(2, 2, 2, places, 512)
    for side in range(2):
        for parity in range(2):
            padded[parity, (half + 1) * side, :, 8 : 8 + places, :] = value[side, parity]

    def put(parity, x, side, col, row):
        y = 8 + places if side else 7
        padded[parity, x, col, y : y + 1, :] = row

    place_sides(put, held, 8 * places, rows)


def shift_leaf(padded, shifted, sign_y, places):
    signs = sign_y[0:1, :].reshape(1, 1, 512)
    for d in range(6):
        step = d - 2
        for parity in range(2):
            found = []
            for target in range(2):
                source = target + (-step if target else step)
                start = 8 + source // 2
                value = padded[parity, :, source % 2, start : start + places, :]
                found.append(value * signs if target else value)
            shifted[d, parity] = jnp.concatenate(found, axis=1).astype(BF16)


def fill_parent(padded, block, doubled, special, rows, width):
    half = rows // 2
    value = project(block[...].reshape(rows * width, DENS), doubled, special).reshape(half, 2, width, 512)
    for parity in range(2):
        padded[parity, 1 : 1 + half, 8 : 8 + width, :] = value[:, parity]
    zero = jnp.zeros((half + 2, 8, 512), F32)
    for parity in range(2):
        padded[parity, :, 0:8, :] = zero
        padded[parity, :, 8 + width : 16 + width, :] = zero


def fill_parent_sides(padded, held, rows, width):
    half = rows // 2
    value = held[0 : 4 * width, :].reshape(2, 2, width, 512)
    for side in range(2):
        for parity in range(2):
            padded[parity, (half + 1) * side, 8 : 8 + width, :] = value[side, parity]

    def put(parity, x, side, col, row):
        y = 8 + width + col if side else 6 + col
        padded[parity, x, y : y + 1, :] = row

    place_sides(put, held, 4 * width, rows)


def shift_parent(padded, shifted, sign_y, width):
    row = lax.broadcasted_iota(jnp.int32, (padded.shape[1], width, 512), 1)
    even = lax.rem(row, 2) == 0
    signs = sign_y[0:1, :].reshape(1, 1, 512)
    for d in range(6):
        step = d - 2
        for parity in range(2):
            forward = padded[parity, :, 8 + step : 8 + step + width, :]
            backward = padded[parity, :, 8 - step : 8 - step + width, :] * signs
            shifted[d, parity] = jnp.where(even, forward, backward)


def leaf_flags(lists, picks, rows, width):
    half, places = rows // 2, width // 2
    block = lists[...].astype(F32).reshape(half, 2, places, 2, len(ALL_OFFSETS))
    found = []
    for cx in range(2):
        pair = []
        for cy in range(2):
            part = block[:, cx, :, cy, :].reshape(half * places, len(ALL_OFFSETS)).astype(BF16)
            pair.append(mm(part, picks[cx, cy]).reshape(half, places, 128))
        found.append(jnp.concatenate(pair, axis=1))
    return found


def parent_flags(lists, picks, rows, width):
    half = rows // 2
    block = lists[...].astype(F32).reshape(half, 2, width, len(ALL_OFFSETS))
    even = lax.rem(lax.broadcasted_iota(jnp.int32, (half, width, 128), 1), 2) == 0
    found = []
    for cx in range(2):
        part = block[:, cx].reshape(half * width, len(ALL_OFFSETS)).astype(BF16)
        pair = [mm(part, picks[cx, cy]).reshape(half, width, 128) for cy in range(2)]
        found.append(jnp.where(even, pair[0], pair[1]))
    return found


def interact(levels, weights, total, group, between=()):
    for first in range(0, COUNT, group):
        last = min(first + group, COUNT)
        parts = [[], []]
        for k in range(first, last):
            a, b = EVEN_OFFSETS[k]
            pieces = [[] for _ in range(4)]
            for shifted, flags, half, width in levels:
                for cx in range(2):
                    source = cx + (-a if cx else a)
                    parity, start = source % 2, source // 2 + 1
                    flag = flags[cx, :, :, k : k + 1]
                    flag = jnp.broadcast_to(flag, (half, width, 128)).astype(shifted.dtype)
                    for t in range(4):
                        mask = -flag if (cx and t % 2) else flag
                        piece = shifted[b + 2, parity, start : start + half, :, lanes(t)] * mask
                        pieces[t].append(piece.reshape(half * width, 128).astype(BF16))
            for t in range(4):
                parts[t // 2].append(jnp.concatenate(pieces[t], axis=0))
        for z in range(2):
            term = mm(jnp.concatenate(parts[z], axis=1), weights[z, first * 256 : last * 256, :])
            cols = slice(256 * z, 256 * z + 256)
            if first == 0:
                total[:, cols] = term
            else:
                total[:, cols] += term
        if first // group < len(between):
            between[first // group]()


def near_body(
    sizes,
    leaf_hbm, parent_in_hbm, leaf_lists_hbm, parent_lists_hbm, up_hbm, down_hbm, inverse_hbm,
    weights_hbm, doubled_hbm, special_hbm, doubled_t_hbm, special_t_hbm, sign_hbm, picks_hbm,
    leaf_check, parent_up, inverse_high, inverse_low,
    leaf, parent_in, leaf_lists, parent_lists, up, down, inverse,
    weights, doubled, special, doubled_t, special_t, sign_y, picks,
    down_high, down_low,
    leaf_strips, leaf_corners, leaf_got_x, leaf_got_y, leaf_got_c, leaf_held,
    parent_strips, parent_corners, parent_got_x, parent_got_y, parent_got_c, parent_held,
    children, leaf_padded, leaf_shifted, leaf_marks,
    parent_padded, parent_shifted, parent_marks, parent_local, total,
    load_sem, leaf_send, leaf_recv, parent_send, parent_recv,
):
    rows, width, prows, pwidth, gx_size, gy_size = sizes
    half, phalf = rows // 2, prows // 2
    places = width // 2
    gx, gy = lax.axis_index("gx"), lax.axis_index("gy")
    ids = [
        (lax.rem(gx + dx + gx_size, gx_size), lax.rem(gy + dy + gy_size, gy_size)) for dx, dy in DIRECTIONS
    ]
    barrier = pltpu.get_barrier_semaphore()
    inside = [
        (gx + dx >= 0) & (gx + dx < gx_size) & (gy + dy >= 0) & (gy + dy < gy_size) for dx, dy in DIRECTIONS
    ]
    count = sum(here.astype(jnp.int32) for here in inside)

    def each(action):
        for n, here in enumerate(inside):
            pl.when(here)(functools.partial(action, n))

    for got in (leaf_got_x, leaf_got_y, leaf_got_c, parent_got_x, parent_got_y, parent_got_c):
        got[...] = jnp.zeros_like(got)
    each(lambda n: pl.semaphore_signal(barrier, inc=1, device_id=ids[n], device_id_type=MESH))

    pairs = [(leaf_hbm, leaf)]
    pairs += [(up_hbm.at[c], up.at[c]) for c in range(4)]
    pairs += [(doubled_hbm, doubled), (special_hbm, special), (sign_hbm, sign_y), (picks_hbm, picks)]
    pairs += [(leaf_lists_hbm, leaf_lists), (parent_lists_hbm, parent_lists)]
    pairs += [(down_hbm, down), (inverse_hbm, inverse), (weights_hbm, weights)]
    pairs += [(doubled_t_hbm, doubled_t), (special_t_hbm, special_t), (parent_in_hbm, parent_in)]
    loads = [pltpu.make_async_copy(a, b, load_sem.at[n]) for n, (a, b) in enumerate(pairs)]
    for load in loads:
        load.start()

    loads[0].wait()
    for cy in range(2):
        children[:, cy] = leaf[...].reshape(rows, places, 2, DENS)[:, :, cy, :]
    pack_sides(lambda x, y: leaf[x, y : y + 1, :], leaf_strips, leaf_corners, rows, width)
    pl.semaphore_wait(barrier, count)
    leaf_copies = side_copies(
        children, leaf_strips, leaf_corners, leaf_got_x, leaf_got_y, leaf_got_c, leaf_send, leaf_recv, rows, ids
    )
    each(lambda n: leaf_copies[n].start())
    for c in range(4):
        loads[1 + c].wait()
        child = children[...].reshape(prows, 2, 2, pwidth, DENS)[:, c // 2, c % 2].reshape(prows * pwidth, DENS)
        term = product(child, *split(up[c])).reshape(prows, pwidth, DENS)
        if c == 0:
            parent_up[...] = term
        else:
            parent_up[...] += term
    pack_sides(lambda x, y: parent_up[x, y : y + 1, :], parent_strips, parent_corners, prows, pwidth)
    parent_copies = side_copies(
        parent_up, parent_strips, parent_corners, parent_got_x, parent_got_y, parent_got_c,
        parent_send, parent_recv, prows, ids,
    )
    each(lambda n: parent_copies[n].start())

    for load in loads[5:13]:
        load.wait()
    basis = (doubled[...], special[...])
    fill_leaf(leaf_padded, children, *basis, rows, 3)
    fill_parent(parent_padded, parent_up, *basis, prows, pwidth)
    for cx, value in enumerate(leaf_flags(leaf_lists, picks, rows, width)):
        leaf_marks[cx] = value
    for cx, value in enumerate(parent_flags(parent_lists, picks, prows, pwidth)):
        parent_marks[cx] = value
    for load in loads[13:]:
        load.wait()
    each(functools.partial(finish, leaf_copies))
    project_sides(leaf_held, leaf_got_x, leaf_got_y, leaf_got_c, *basis)
    fill_leaf_sides(leaf_padded, leaf_held, rows, places)
    shift_leaf(leaf_padded, leaf_shifted, sign_y, places)
    each(functools.partial(finish, parent_copies))
    project_sides(parent_held, parent_got_x, parent_got_y, parent_got_c, *basis)
    fill_parent_sides(parent_padded, parent_held, prows, pwidth)
    shift_parent(parent_padded, parent_shifted, sign_y, pwidth)
    levels = [(leaf_shifted, leaf_marks, half, width), (parent_shifted, parent_marks, phalf, pwidth)]

    def split_down(c):
        down_high[c], down_low[c] = split(down[c])

    def split_inverse():
        inverse_high[...], inverse_low[...] = split(inverse[...])

    interact(levels, weights, total, 3, [functools.partial(split_down, c) for c in range(4)] + [split_inverse])

    signs = sign_y[0:1, :].reshape(1, 1, 512)
    leaf_count, parent_count = rows * width, prows * pwidth
    y = total[leaf_count : leaf_count + parent_count, :].reshape(2, phalf, pwidth, 512)
    row = lax.broadcasted_iota(jnp.int32, (phalf, pwidth, 512), 1)
    y = [jnp.where(lax.rem(row, 2) == 0, part, part * signs) for part in (y[0], y[1] * turned((1, 1, 512)))]
    y = jnp.concatenate(y, axis=0).reshape(parent_count, 512)
    value = product(expand(y, doubled_t[...], special_t[...]), inverse_high[...], inverse_low[...])
    value = value.reshape(2, phalf, pwidth, DENS)
    for cx in range(2):
        for i in range(phalf):
            parent_local[2 * i + cx] = value[cx, i] + parent_in[2 * i + cx]

    quarter = leaf_count // 4
    for c in range(4):
        y = total[c * quarter : (c + 1) * quarter, :].reshape(half // 2, 2, places, 512)
        if c >= 2:
            y = y * turned((1, 1, 1, 512))
        y = jnp.concatenate([y[:, 0:1], y[:, 1:2] * signs.reshape(1, 1, 1, 512)], axis=1).reshape(quarter, 512)
        value = expand(y, doubled_t[...], special_t[...]).reshape(half // 2, 2, places, DENS)
        for i in range(half // 2):
            leaf_check[2 * (i + (c % 2) * (half // 2)) + c // 2] = value[i]

    local = parent_local[...].reshape(parent_count, DENS)
    for c in range(4):
        value = product(local, down_high[c], down_low[c]).reshape(prows, pwidth, DENS)
        for i in range(prows):
            leaf_check[2 * i + c // 2, c % 2] += value[i]


def last_body(check, parent_up, high, low, leaf_down_hbm, parent_up_hbm, leaf_down, sem):
    rows, _, places, _ = check.shape
    copies = [pltpu.make_async_copy(parent_up, parent_up_hbm, sem.at[0])]
    copies[0].start()
    part = rows // 2
    for c in range(2):
        here = slice(part * c, part * c + part)
        value = product(check[here].reshape(part * 2 * places, DENS), high[...], low[...])
        value = value.reshape(part, 2, places, DENS)
        pair = [value[:, cy].reshape(part, places, 1, DENS) for cy in range(2)]
        leaf_down[here] = jnp.concatenate(pair, axis=2).reshape(part, 2 * places, DENS)
        copies.append(pltpu.make_async_copy(leaf_down.at[here], leaf_down_hbm.at[here], sem.at[1 + c]))
        copies[-1].start()
    for copy in copies:
        copy.wait()


def local(sizes, leaf_up, parent_in, leaf_lists, parent_lists, up_transfer, down_transfer, check_inverse):
    rows, width, prows, pwidth = sizes[:4]
    half, phalf = rows // 2, prows // 2
    places = width // 2
    names = ("weights", "doubled", "special", "doubled_t", "special_t", "sign_y", "picks")
    constants = [jnp.asarray(tables()[name]) for name in names]
    operands = [leaf_up, parent_in, leaf_lists, parent_lists, up_transfer, down_transfer, check_inverse] + constants
    scratch = [pltpu.VMEM(x.shape, x.dtype) for x in operands]
    scratch += [pltpu.VMEM((4, DENS, DENS), BF16)] * 2

    def sides(x_shape, rows_here, total):
        return [
            pltpu.VMEM((2, 2 * rows_here, DENS), F32),
            pltpu.VMEM((2, 2, 4, DENS), F32),
            pltpu.VMEM((2, 2) + x_shape + (DENS,), F32),
            pltpu.VMEM((2, 2 * rows_here, DENS), F32),
            pltpu.VMEM((2, 2, 4, DENS), F32),
            pltpu.VMEM((total, 512), F32),
        ]

    scratch += sides((2, places), rows, 4 * width + 4 * rows + 16)
    scratch += sides((pwidth,), prows, 4 * pwidth + 4 * prows + 16)
    scratch += [
        pltpu.VMEM((rows, 2, places, DENS), F32),
        pltpu.VMEM((2, half + 2, 2, 16 + places, 512), F32),
        pltpu.VMEM((6, 2, half + 2, width, 512), BF16),
        pltpu.VMEM((2, half, width, 128), F32),
        pltpu.VMEM((2, phalf + 2, 16 + pwidth, 512), F32),
        pltpu.VMEM((6, 2, phalf + 2, pwidth, 512), F32),
        pltpu.VMEM((2, phalf, pwidth, 128), F32),
        pltpu.VMEM((prows, pwidth, DENS), F32),
        pltpu.VMEM((rows * width + prows * pwidth, 512), F32),
        pltpu.SemaphoreType.DMA((17,)),
        pltpu.SemaphoreType.DMA((8,)),
        pltpu.SemaphoreType.DMA((8,)),
        pltpu.SemaphoreType.DMA((8,)),
        pltpu.SemaphoreType.DMA((8,)),
    ]
    check, parent_up, high, low = pl.pallas_call(
        functools.partial(near_body, sizes),
        out_shape=(
            pltpu.VMEM((rows, 2, places, DENS), F32),
            pltpu.VMEM((prows, pwidth, DENS), F32),
            pltpu.VMEM((DENS, DENS), BF16),
            pltpu.VMEM((DENS, DENS), BF16),
        ),
        in_specs=[pl.BlockSpec(memory_space=pltpu.HBM)] * len(operands),
        out_specs=(pl.BlockSpec(memory_space=pltpu.VMEM),) * 4,
        scratch_shapes=scratch,
        compiler_params=pltpu.CompilerParams(
            collective_id=0, has_side_effects=True, vmem_limit_bytes=60 * 1024 * 1024
        ),
    )(*operands)
    return pl.pallas_call(
        last_body,
        out_shape=(
            jax.ShapeDtypeStruct((rows, width, DENS), F32),
            jax.ShapeDtypeStruct((prows, pwidth, DENS), F32),
        ),
        in_specs=[pl.BlockSpec(memory_space=pltpu.VMEM)] * 4,
        out_specs=(pl.BlockSpec(memory_space=pltpu.HBM),) * 2,
        scratch_shapes=[pltpu.VMEM((rows, width, DENS), F32), pltpu.SemaphoreType.DMA((3,))],
        compiler_params=pltpu.CompilerParams(vmem_limit_bytes=16 * 1024 * 1024),
    )(check, parent_up, high, low)


def solution(mesh):
    gx_size, gy_size = mesh.shape["gx"], mesh.shape["gy"]
    sizes = (192 // gx_size, 256 // gy_size, 96 // gx_size, 128 // gy_size, gx_size, gy_size)
    placed = (P("gx", "gy", None),) * 4 + (P(), P(), P())
    return jax.shard_map(
        functools.partial(local, sizes),
        mesh=mesh,
        in_specs=placed,
        out_specs=(P("gx", "gy", None), P("gx", "gy", None)),
        check_vma=False,
    )
```

```python
import functools
import itertools

import jax
import jax.numpy as jnp
import ml_dtypes
import numpy as np
from jax import lax
from jax.experimental import pallas as pl
from jax.experimental.pallas import tpu as pltpu
from jax.sharding import PartitionSpec as P

ORDER = 6
DENS = 456
TOP = 14
F32 = jnp.float32
BF16 = jnp.bfloat16
MESH = pl.DeviceIdType.MESH

ALL_OFFSETS = [(a, b) for a in range(-3, 4) for b in range(-3, 4) if max(abs(a), abs(b)) >= 2]
EVEN_OFFSETS = [
    (a, b)
    for steps in ((-2, -1), (0, 1), (2, 3))
    for a in range(-2, 4)
    for b in steps
    if max(abs(a), abs(b)) >= 2
]
COUNT = len(EVEN_OFFSETS)


def rounded(values):
    return values.astype(ml_dtypes.bfloat16).astype(np.float64)


def surface_points():
    grid_line = np.linspace(-1.0, 1.0, ORDER)
    points = []
    for i in range(ORDER):
        for j in range(ORDER):
            for k in range(ORDER):
                if min(i, j, k) == 0 or max(i, j, k) == ORDER - 1:
                    points.append((grid_line[i], grid_line[j], grid_line[k]))
    return np.array(points)


def kernel_matrix(points, shift):
    r = 0.525 * (points[:, None, :] - points[None, :, :]) - np.array([shift[0], shift[1], 0.0])
    length = np.sqrt((r * r).sum(-1))
    count = len(points)
    matrix = np.zeros((3, count, 3, count))
    for a in range(3):
        for b in range(3):
            matrix[a, :, b, :] = (float(a == b) / length + r[..., a] * r[..., b] / length**3) / (8.0 * np.pi)
    return matrix.reshape(3 * count, 3 * count)


def mirror_basis(points, signs):
    count = len(points)
    place = {tuple(np.round(p * (ORDER - 1)).astype(int)): i for i, p in enumerate(points)}
    corner = [i for i, p in enumerate(points) if (p > 0).all()]
    basis = np.zeros((3 * count, 3 * len(corner)))
    for a in range(3):
        for h, i in enumerate(corner):
            for flip in itertools.product([1, -1], repeat=3):
                j = place[tuple(np.round(points[i] * np.array(flip) * (ORDER - 1)).astype(int))]
                sign = 1
                for axis in range(3):
                    if flip[axis] == -1:
                        sign *= signs[axis] * (-1 if axis == a else 1)
                basis[a * count + j, a * len(corner) + h] = sign
    return basis / np.sqrt(8.0)


@functools.lru_cache(maxsize=1)
def tables():
    points = surface_points()
    kernels = {o: kernel_matrix(points, o) for o in ALL_OFFSETS}
    stacked = np.concatenate([kernels[o] for o in ALL_OFFSETS], axis=1)
    basis = np.zeros((DENS, 512))
    sign_y = np.ones(512)
    high, low, main = [], [], []
    for t, (sx, sz) in enumerate([(1, 1), (-1, 1), (1, -1), (-1, -1)]):
        found = []
        for sy in (1, -1):
            mirror = mirror_basis(points, (sx, sy, sz))
            left, size, _ = np.linalg.svd(mirror.T @ stacked, full_matrices=False)
            for j in range(left.shape[1]):
                found.append((size[j], sy, rounded(mirror @ left[:, j])))
        found.sort(key=lambda item: -item[0])
        start = 128 * t + 32 * t
        special = range(start, start + 2 * TOP)
        rest = [lane for lane in range(128 * t, 128 * t + 128) if lane not in special]
        for j, (_, sy, column) in enumerate(found):
            lane = start + j if j < TOP else rest[j - TOP]
            basis[:, lane] = column
            sign_y[lane] = sy
            main.append(lane)
            if j < TOP:
                high.append(lane)
                low.append(lane + TOP)
                sign_y[lane + TOP] = sy
    inverse = np.linalg.inv(basis[:, main])
    doubled = basis.copy()
    doubled[:, low] = basis[:, high]
    special = np.zeros((DENS, 128))
    for t in range(4):
        special[:, 32 * t : 32 * t + 2 * TOP] = doubled[:, 160 * t : 160 * t + 2 * TOP]
    weights = np.zeros((2, COUNT, 256, 256), ml_dtypes.bfloat16)
    for k, offset in enumerate(EVEN_OFFSETS):
        core = np.zeros((512, 512))
        core[np.ix_(main, main)] = (inverse @ kernels[offset] @ inverse.T).T
        leading = core[np.ix_(high, high)]
        core[np.ix_(low, high)] = leading
        core[np.ix_(high, low)] = leading - rounded(leading)
        weights[0, k] = core[:256, :256].astype(ml_dtypes.bfloat16)
        weights[1, k] = core[256:, 256:].astype(ml_dtypes.bfloat16)
    picks = np.zeros((2, 2, len(ALL_OFFSETS), 128), ml_dtypes.bfloat16)
    for cx in range(2):
        for cy in range(2):
            for k, (a, b) in enumerate(EVEN_OFFSETS):
                offset = (-a if cx else a, -b if cy else b)
                picks[cx, cy, ALL_OFFSETS.index(offset), k] = 1
    return {
        "weights": weights.reshape(2, COUNT * 256, 256),
        "doubled": doubled.astype(ml_dtypes.bfloat16),
        "special": special.astype(ml_dtypes.bfloat16),
        "doubled_t": np.ascontiguousarray(doubled.T).astype(ml_dtypes.bfloat16),
        "special_t": np.ascontiguousarray(special.T).astype(ml_dtypes.bfloat16),
        "sign_y": np.tile(sign_y[None, :], (8, 1)).astype(np.float32),
        "picks": picks,
    }


def split(value):
    high = value.astype(BF16)
    return high, (value - high.astype(F32)).astype(BF16)


def mm(a, b):
    return jnp.dot(a, b, preferred_element_type=F32)


def mm_t(a, b):
    return lax.dot_general(a, b, (((1,), (1,)), ((), ())), preferred_element_type=F32)


def product(rows, high_matrix, low_matrix):
    count = rows.shape[0]
    high, low = split(rows)
    both = mm_t(jnp.concatenate([high, low], axis=0), high_matrix)
    return both[:count] + both[count:] + mm_t(high, low_matrix)


def lanes(t):
    return slice(128 * t, 128 * t + 128)


def lane_index(shape):
    return lax.broadcasted_iota(jnp.int32, shape, len(shape) - 1)


def project(rows, doubled, special):
    high, low = split(rows)
    main = mm(high, doubled)
    fine = mm(low, special)
    place = lane_index(fine.shape)
    tiles = []
    for t in range(4):
        tile = main[:, lanes(t)]
        tile = jnp.where((place >= 32 * t) & (place < 32 * t + 32), tile + fine, tile)
        left_over = tile - tile.astype(BF16).astype(F32)
        tiles.append(jnp.where((place >= 32 * t + TOP) & (place < 32 * t + 2 * TOP), left_over, tile))
    return jnp.concatenate(tiles, axis=1)


def expand(y, doubled_t, special_t):
    high = y.astype(BF16)
    rest = y - high.astype(F32)
    place = lane_index((y.shape[0], 128))
    fine = jnp.zeros((y.shape[0], 128), F32)
    for t in range(4):
        fine = jnp.where((place >= 32 * t) & (place < 32 * t + 32), rest[:, lanes(t)], fine)
    return mm(high, doubled_t) + mm(fine.astype(BF16), special_t)


def turned(shape):
    return jnp.where(lax.rem(lax.div(lane_index(shape), 128), 2) == 1, -1.0, 1.0)


DIRECTIONS = [(0, -1), (0, 1), (-1, -1), (-1, 1), (1, -1), (1, 1), (-1, 0), (1, 0)]


def pack_sides(row_of, strips, corners, rows, width):
    half = rows // 2
    for side in range(2):
        for col in range(2):
            y = (width - 2 if side else 0) + col
            for parity in range(2):
                for i in range(half):
                    at = col * rows + parity * half + i
                    strips[side, at : at + 1, :] = row_of(2 * i + parity, y)
    for sx in range(2):
        for sy in range(2):
            for col in range(2):
                y = (width - 2 if sy else 0) + col
                for parity in range(2):
                    x = (rows - 2 if sx else 0) + parity
                    at = 2 * col + parity
                    corners[sx, sy, at : at + 1, :] = row_of(x, y)


def side_copies(block, strips, corners, got_x, got_y, got_c, send, recv, rows, ids):
    copies = []
    for n, (dx, dy) in enumerate(DIRECTIONS):
        sx, sy = (dx + 1) // 2, (dy + 1) // 2
        if dy == 0:
            source = block.at[rows - 2 : rows] if dx > 0 else block.at[0:2]
            target = got_x.at[1 - sx]
        elif dx == 0:
            source, target = strips.at[sy], got_y.at[1 - sy]
        else:
            source, target = corners.at[sx, sy], got_c.at[1 - sx, 1 - sy]
        copies.append(
            pltpu.make_async_remote_copy(
                src_ref=source,
                dst_ref=target,
                send_sem=send.at[n],
                recv_sem=recv.at[n],
                device_id=ids[n],
                device_id_type=MESH,
            )
        )
    return copies


def finish(copies, n):
    dx, dy = DIRECTIONS[n]
    copies[n].wait_send()
    copies[DIRECTIONS.index((-dx, -dy))].wait_recv()


def project_sides(got_x, got_y, got_c, doubled, special):
    parts = [got_x[...].reshape(-1, DENS)] if got_x is not None else []
    parts += [got_y[...].reshape(-1, DENS)]
    parts += [got_c[sx, sy] for sx in range(2) for sy in range(2)]
    return project(jnp.concatenate(parts, axis=0), doubled, special)


def place_sides(put, held, first, rows):
    half = rows // 2
    for side in range(2):
        for col in range(2):
            for parity in range(2):
                for i in range(half):
                    at = first + (side * 2 + col) * rows + parity * half + i
                    put(parity, 1 + i, side, col, held[at : at + 1, :])
                for sx in range(2):
                    at = first + 4 * rows + (sx * 2 + side) * 4 + 2 * col + parity
                    put(parity, (half + 1) * sx, side, col, held[at : at + 1, :])


def fill_leaf(padded, children, doubled, special, rows, chunk):
    half = rows // 2
    places = children.shape[2]
    for c in range(0, half, chunk):
        value = children[2 * c : 2 * c + 2 * chunk].reshape(4 * chunk * places, DENS)
        value = project(value, doubled, special).reshape(chunk, 2, 2, places, 512)
        for parity in range(2):
            padded[parity, 1 + c : 1 + c + chunk, :, 8 : 8 + places, :] = value[:, parity]


def fill_leaf_x(padded, got_x, doubled, special, rows, places):
    half = rows // 2
    value = project(got_x[...].reshape(8 * places, DENS), doubled, special).reshape(2, 2, places, 2, 512)
    for side in range(2):
        for parity in range(2):
            for cy in range(2):
                padded[parity, (half + 1) * side, cy, 8 : 8 + places, :] = value[side, parity, :, cy]


def fill_leaf_y(padded, held, rows, places):
    def put(parity, x, side, col, row):
        y = 8 + places if side else 7
        padded[parity, x, col, y : y + 1, :] = row

    place_sides(put, held, 0, rows)


def shift_leaf(padded, shifted, sign_y, places, steps):
    signs = sign_y[0:1, :].reshape(1, 1, 512)
    for step in steps:
        d = step + 2
        for parity in range(2):
            found = []
            for target in range(2):
                source = target + (-step if target else step)
                start = 8 + source // 2
                value = padded[parity, :, source % 2, start : start + places, :]
                found.append(value * signs if target else value)
            shifted[d, parity] = jnp.concatenate(found, axis=1).astype(BF16)


def fill_parent(padded, block, doubled, special, rows, width):
    half = rows // 2
    value = project(block[...].reshape(rows * width, DENS), doubled, special).reshape(half, 2, width, 512)
    for parity in range(2):
        padded[parity, 1 : 1 + half, 8 : 8 + width, :] = value[:, parity]
    zero = jnp.zeros((half + 2, 8, 512), F32)
    for parity in range(2):
        padded[parity, :, 0:8, :] = zero
        padded[parity, :, 8 + width : 16 + width, :] = zero


def fill_parent_sides(padded, held, rows, width):
    half = rows // 2
    value = held[0 : 4 * width, :].reshape(2, 2, width, 512)
    for side in range(2):
        for parity in range(2):
            padded[parity, (half + 1) * side, 8 : 8 + width, :] = value[side, parity]

    def put(parity, x, side, col, row):
        y = 8 + width + col if side else 6 + col
        padded[parity, x, y : y + 1, :] = row

    place_sides(put, held, 4 * width, rows)


def shift_parent(padded, shifted, sign_y, width):
    row = lax.broadcasted_iota(jnp.int32, (padded.shape[1], width, 512), 1)
    even = lax.rem(row, 2) == 0
    signs = sign_y[0:1, :].reshape(1, 1, 512)
    for d in range(6):
        step = d - 2
        for parity in range(2):
            forward = padded[parity, :, 8 + step : 8 + step + width, :]
            backward = padded[parity, :, 8 - step : 8 - step + width, :] * signs
            shifted[d, parity] = jnp.where(even, forward, backward)


def leaf_flags(lists, picks, rows, width):
    half, places = rows // 2, width // 2
    block = lists[...].astype(F32).reshape(half, 2, places, 2, len(ALL_OFFSETS))
    found = []
    for cx in range(2):
        pair = []
        for cy in range(2):
            part = block[:, cx, :, cy, :].reshape(half * places, len(ALL_OFFSETS)).astype(BF16)
            pair.append(mm(part, picks[cx, cy]).reshape(half, places, 128))
        found.append(jnp.concatenate(pair, axis=1))
    return found


def parent_flags(lists, picks, rows, width):
    half = rows // 2
    block = lists[...].astype(F32).reshape(half, 2, width, len(ALL_OFFSETS))
    even = lax.rem(lax.broadcasted_iota(jnp.int32, (half, width, 128), 1), 2) == 0
    found = []
    for cx in range(2):
        part = block[:, cx].reshape(half * width, len(ALL_OFFSETS)).astype(BF16)
        pair = [mm(part, picks[cx, cy]).reshape(half, width, 128) for cy in range(2)]
        found.append(jnp.where(even, pair[0], pair[1]))
    return found


GROUPS = [tuple(range(first, first + 3)) for first in range(0, COUNT, 3)]


def block_pieces(shifted, flags, half, width, k):
    a, b = EVEN_OFFSETS[k]
    pieces = [[] for _ in range(4)]
    for cx in range(2):
        source = cx + (-a if cx else a)
        parity, start = source % 2, source // 2 + 1
        flag = jnp.broadcast_to(flags[cx, :, :, k : k + 1], (half, width, 128)).astype(shifted.dtype)
        for t in range(4):
            mask = -flag if (cx and t % 2) else flag
            piece = shifted[b + 2, parity, start : start + half, :, lanes(t)] * mask
            pieces[t].append(piece.reshape(half * width, 128).astype(BF16))
    return [jnp.concatenate(piece, axis=0) for piece in pieces]


def interact(group, weights, levels):
    parts = [[], []]
    for k in group:
        found = [level[0](k) for level in levels]
        for t in range(4):
            parts[t // 2].append(jnp.concatenate([one[t] for one in found], axis=0))
    for z in range(2):
        rows = slice(256 * group[0], 256 * group[-1] + 256)
        term = mm(jnp.concatenate(parts[z], axis=1), weights[z, rows, :])
        cols = slice(256 * z, 256 * z + 256)
        at = 0
        for _, count, total, first in levels:
            if first:
                total[:, cols] = term[at : at + count]
            else:
                total[:, cols] += term[at : at + count]
            at += count


def near_body(
    sizes,
    leaf_hbm, parent_in_hbm, leaf_lists_hbm, parent_lists_hbm, up_hbm, down_hbm, inverse_hbm,
    weights_hbm, doubled_hbm, special_hbm, doubled_t_hbm, special_t_hbm, sign_hbm, picks_hbm,
    leaf_check, parent_up, inverse_high, inverse_low,
    leaf, parent_in, leaf_lists, parent_lists, up, down, inverse,
    weights, doubled, special, doubled_t, special_t, sign_y, picks,
    down_high, down_low,
    leaf_strips, leaf_corners, leaf_got_x, leaf_got_y, leaf_got_c, leaf_held,
    parent_strips, parent_corners, parent_got_x, parent_got_y, parent_got_c, parent_held,
    children, leaf_padded, leaf_shifted, leaf_marks,
    parent_padded, parent_shifted, parent_marks, parent_local, leaf_total, parent_total,
    load_sem, leaf_send, leaf_recv, parent_send, parent_recv,
):
    rows, width, prows, pwidth, gx_size, gy_size = sizes
    half, phalf = rows // 2, prows // 2
    places = width // 2
    gx, gy = lax.axis_index("gx"), lax.axis_index("gy")
    ids = [
        (lax.rem(gx + dx + gx_size, gx_size), lax.rem(gy + dy + gy_size, gy_size)) for dx, dy in DIRECTIONS
    ]
    barrier = pltpu.get_barrier_semaphore()
    inside = [
        (gx + dx >= 0) & (gx + dx < gx_size) & (gy + dy >= 0) & (gy + dy < gy_size) for dx, dy in DIRECTIONS
    ]
    count = sum(here.astype(jnp.int32) for here in inside)

    def each(action, first=0, last=len(DIRECTIONS)):
        for n in range(first, last):
            pl.when(inside[n])(functools.partial(action, n))

    for got in (leaf_got_x, leaf_got_y, leaf_got_c, parent_got_x, parent_got_y, parent_got_c):
        got[...] = jnp.zeros_like(got)
    each(lambda n: pl.semaphore_signal(barrier, inc=1, device_id=ids[n], device_id_type=MESH))

    pairs = [(leaf_hbm, leaf)]
    pairs += [(up_hbm.at[c], up.at[c]) for c in range(4)]
    pairs += [(doubled_hbm, doubled), (special_hbm, special), (sign_hbm, sign_y), (picks_hbm, picks)]
    pairs += [(leaf_lists_hbm, leaf_lists), (parent_lists_hbm, parent_lists)]
    pairs += [(down_hbm, down), (inverse_hbm, inverse), (weights_hbm, weights)]
    pairs += [(doubled_t_hbm, doubled_t), (special_t_hbm, special_t), (parent_in_hbm, parent_in)]
    loads = [pltpu.make_async_copy(a, b, load_sem.at[n]) for n, (a, b) in enumerate(pairs)]
    for load in loads:
        load.start()

    loads[0].wait()
    pack_sides(lambda x, y: leaf[x, y : y + 1, :], leaf_strips, leaf_corners, rows, width)
    pl.semaphore_wait(barrier, count)
    leaf_copies = side_copies(
        leaf, leaf_strips, leaf_corners, leaf_got_x, leaf_got_y, leaf_got_c, leaf_send, leaf_recv, rows, ids
    )
    each(lambda n: leaf_copies[n].start())
    for cy in range(2):
        children[:, cy] = leaf[...].reshape(rows, places, 2, DENS)[:, :, cy, :]
    for c in range(4):
        loads[1 + c].wait()
        child = children[...].reshape(prows, 2, 2, pwidth, DENS)[:, c // 2, c % 2].reshape(prows * pwidth, DENS)
        term = product(child, *split(up[c])).reshape(prows, pwidth, DENS)
        if c == 0:
            parent_up[...] = term
        else:
            parent_up[...] += term
    pack_sides(lambda x, y: parent_up[x, y : y + 1, :], parent_strips, parent_corners, prows, pwidth)
    parent_copies = side_copies(
        parent_up, parent_strips, parent_corners, parent_got_x, parent_got_y, parent_got_c,
        parent_send, parent_recv, prows, ids,
    )
    each(lambda n: parent_copies[n].start())

    for load in loads[5:13]:
        load.wait()
    basis = (doubled[...], special[...])
    fill_leaf(leaf_padded, children, *basis, rows, 3)
    fill_parent(parent_padded, parent_up, *basis, prows, pwidth)
    for cx, value in enumerate(leaf_flags(leaf_lists, picks, rows, width)):
        leaf_marks[cx] = value
    for cx, value in enumerate(parent_flags(parent_lists, picks, prows, pwidth)):
        parent_marks[cx] = value
    for load in loads[13:]:
        load.wait()
    each(functools.partial(finish, leaf_copies), 6)
    fill_leaf_x(leaf_padded, leaf_got_x, *basis, rows, places)
    shift_leaf(leaf_padded, leaf_shifted, sign_y, places, (0, 1))
    leaf_pieces = functools.partial(block_pieces, leaf_shifted, leaf_marks, half, width)
    for group in GROUPS[3:5]:
        interact(group, weights, [(leaf_pieces, rows * width, leaf_total, group == GROUPS[3])])

    each(functools.partial(finish, leaf_copies), 0, 6)
    leaf_held[...] = project_sides(None, leaf_got_y, leaf_got_c, *basis)
    fill_leaf_y(leaf_padded, leaf_held, rows, places)
    shift_leaf(leaf_padded, leaf_shifted, sign_y, places, (-2, -1, 2, 3))
    each(functools.partial(finish, parent_copies))
    parent_held[...] = project_sides(parent_got_x, parent_got_y, parent_got_c, *basis)
    fill_parent_sides(parent_padded, parent_held, prows, pwidth)
    shift_parent(parent_padded, parent_shifted, sign_y, pwidth)
    parent_pieces = functools.partial(block_pieces, parent_shifted, parent_marks, phalf, pwidth)
    for turn, group in enumerate(GROUPS[:3] + GROUPS[5:]):
        levels = [(leaf_pieces, rows * width, leaf_total, False)]
        interact(group, weights, levels + [(parent_pieces, prows * pwidth, parent_total, turn == 0)])
        if turn < 4:
            down_high[turn], down_low[turn] = split(down[turn])
        elif turn == 4:
            inverse_high[...], inverse_low[...] = split(inverse[...])
    for group in GROUPS[3:5]:
        interact(group, weights, [(parent_pieces, prows * pwidth, parent_total, False)])

    signs = sign_y[0:1, :].reshape(1, 1, 512)
    leaf_count, parent_count = rows * width, prows * pwidth
    y = parent_total[...].reshape(2, phalf, pwidth, 512)
    row = lax.broadcasted_iota(jnp.int32, (phalf, pwidth, 512), 1)
    y = [jnp.where(lax.rem(row, 2) == 0, part, part * signs) for part in (y[0], y[1] * turned((1, 1, 512)))]
    y = jnp.concatenate(y, axis=0).reshape(parent_count, 512)
    value = product(expand(y, doubled_t[...], special_t[...]), inverse_high[...], inverse_low[...])
    value = value.reshape(2, phalf, pwidth, DENS)
    for cx in range(2):
        for i in range(phalf):
            parent_local[2 * i + cx] = value[cx, i] + parent_in[2 * i + cx]

    quarter = leaf_count // 4
    for c in range(4):
        y = leaf_total[c * quarter : (c + 1) * quarter, :].reshape(half // 2, 2, places, 512)
        if c >= 2:
            y = y * turned((1, 1, 1, 512))
        y = jnp.concatenate([y[:, 0:1], y[:, 1:2] * signs.reshape(1, 1, 1, 512)], axis=1).reshape(quarter, 512)
        value = expand(y, doubled_t[...], special_t[...]).reshape(half // 2, 2, places, DENS)
        for i in range(half // 2):
            leaf_check[2 * (i + (c % 2) * (half // 2)) + c // 2] = value[i]

    local = parent_local[...].reshape(parent_count, DENS)
    for c in range(4):
        value = product(local, down_high[c], down_low[c]).reshape(prows, pwidth, DENS)
        for i in range(prows):
            leaf_check[2 * i + c // 2, c % 2] += value[i]


def last_body(check, parent_up, high, low, leaf_down_hbm, parent_up_hbm, leaf_down, sem):
    rows, _, places, _ = check.shape
    copies = [pltpu.make_async_copy(parent_up, parent_up_hbm, sem.at[0])]
    copies[0].start()
    part = rows // 2
    for c in range(2):
        here = slice(part * c, part * c + part)
        value = product(check[here].reshape(part * 2 * places, DENS), high[...], low[...])
        value = value.reshape(part, 2, places, DENS)
        pair = [value[:, cy].reshape(part, places, 1, DENS) for cy in range(2)]
        leaf_down[here] = jnp.concatenate(pair, axis=2).reshape(part, 2 * places, DENS)
        copies.append(pltpu.make_async_copy(leaf_down.at[here], leaf_down_hbm.at[here], sem.at[1 + c]))
        copies[-1].start()
    for copy in copies:
        copy.wait()


def local(sizes, leaf_up, parent_in, leaf_lists, parent_lists, up_transfer, down_transfer, check_inverse):
    rows, width, prows, pwidth = sizes[:4]
    half, phalf = rows // 2, prows // 2
    places = width // 2
    names = ("weights", "doubled", "special", "doubled_t", "special_t", "sign_y", "picks")
    constants = [jnp.asarray(tables()[name]) for name in names]
    operands = [leaf_up, parent_in, leaf_lists, parent_lists, up_transfer, down_transfer, check_inverse] + constants
    scratch = [pltpu.VMEM(x.shape, x.dtype) for x in operands]
    scratch += [pltpu.VMEM((4, DENS, DENS), BF16)] * 2

    def sides(x_shape, rows_here, total):
        return [
            pltpu.VMEM((2, 2 * rows_here, DENS), F32),
            pltpu.VMEM((2, 2, 4, DENS), F32),
            pltpu.VMEM((2, 2) + x_shape + (DENS,), F32),
            pltpu.VMEM((2, 2 * rows_here, DENS), F32),
            pltpu.VMEM((2, 2, 4, DENS), F32),
            pltpu.VMEM((total, 512), F32),
        ]

    scratch += sides((width,), rows, 4 * rows + 16)
    scratch += sides((pwidth,), prows, 4 * pwidth + 4 * prows + 16)
    scratch += [
        pltpu.VMEM((rows, 2, places, DENS), F32),
        pltpu.VMEM((2, half + 2, 2, 16 + places, 512), F32),
        pltpu.VMEM((6, 2, half + 2, width, 512), BF16),
        pltpu.VMEM((2, half, width, 128), F32),
        pltpu.VMEM((2, phalf + 2, 16 + pwidth, 512), F32),
        pltpu.VMEM((6, 2, phalf + 2, pwidth, 512), F32),
        pltpu.VMEM((2, phalf, pwidth, 128), F32),
        pltpu.VMEM((prows, pwidth, DENS), F32),
        pltpu.VMEM((rows * width, 512), F32),
        pltpu.VMEM((prows * pwidth, 512), F32),
        pltpu.SemaphoreType.DMA((17,)),
        pltpu.SemaphoreType.DMA((8,)),
        pltpu.SemaphoreType.DMA((8,)),
        pltpu.SemaphoreType.DMA((8,)),
        pltpu.SemaphoreType.DMA((8,)),
    ]
    check, parent_up, high, low = pl.pallas_call(
        functools.partial(near_body, sizes),
        out_shape=(
            pltpu.VMEM((rows, 2, places, DENS), F32),
            pltpu.VMEM((prows, pwidth, DENS), F32),
            pltpu.VMEM((DENS, DENS), BF16),
            pltpu.VMEM((DENS, DENS), BF16),
        ),
        in_specs=[pl.BlockSpec(memory_space=pltpu.HBM)] * len(operands),
        out_specs=(pl.BlockSpec(memory_space=pltpu.VMEM),) * 4,
        scratch_shapes=scratch,
        compiler_params=pltpu.CompilerParams(
            collective_id=0, has_side_effects=True, vmem_limit_bytes=60 * 1024 * 1024
        ),
    )(*operands)
    return pl.pallas_call(
        last_body,
        out_shape=(
            jax.ShapeDtypeStruct((rows, width, DENS), F32),
            jax.ShapeDtypeStruct((prows, pwidth, DENS), F32),
        ),
        in_specs=[pl.BlockSpec(memory_space=pltpu.VMEM)] * 4,
        out_specs=(pl.BlockSpec(memory_space=pltpu.HBM),) * 2,
        scratch_shapes=[pltpu.VMEM((rows, width, DENS), F32), pltpu.SemaphoreType.DMA((3,))],
        compiler_params=pltpu.CompilerParams(vmem_limit_bytes=16 * 1024 * 1024),
    )(check, parent_up, high, low)


def solution(mesh):
    gx_size, gy_size = mesh.shape["gx"], mesh.shape["gy"]
    sizes = (192 // gx_size, 256 // gy_size, 96 // gx_size, 128 // gy_size, gx_size, gy_size)
    placed = (P("gx", "gy", None),) * 4 + (P(), P(), P())
    return jax.shard_map(
        functools.partial(local, sizes),
        mesh=mesh,
        in_specs=placed,
        out_specs=(P("gx", "gy", None), P("gx", "gy", None)),
        check_vma=False,
    )
```

```python
import functools
import itertools

import jax
import jax.numpy as jnp
import ml_dtypes
import numpy as np
from jax import lax
from jax.experimental import pallas as pl
from jax.experimental.pallas import tpu as pltpu
from jax.sharding import PartitionSpec as P

ORDER = 6
DENS = 456
TOP = 14
F32 = jnp.float32
BF16 = jnp.bfloat16
MESH = pl.DeviceIdType.MESH

ALL_OFFSETS = [(a, b) for a in range(-3, 4) for b in range(-3, 4) if max(abs(a), abs(b)) >= 2]
EVEN_OFFSETS = [
    (a, b)
    for steps in ((-2, -1), (0, 1), (2, 3))
    for a in range(-2, 4)
    for b in steps
    if max(abs(a), abs(b)) >= 2
]
COUNT = len(EVEN_OFFSETS)


def rounded(values):
    return values.astype(ml_dtypes.bfloat16).astype(np.float64)


def surface_points():
    grid_line = np.linspace(-1.0, 1.0, ORDER)
    points = []
    for i in range(ORDER):
        for j in range(ORDER):
            for k in range(ORDER):
                if min(i, j, k) == 0 or max(i, j, k) == ORDER - 1:
                    points.append((grid_line[i], grid_line[j], grid_line[k]))
    return np.array(points)


def kernel_matrix(points, shift):
    r = 0.525 * (points[:, None, :] - points[None, :, :]) - np.array([shift[0], shift[1], 0.0])
    length = np.sqrt((r * r).sum(-1))
    count = len(points)
    matrix = np.zeros((3, count, 3, count))
    for a in range(3):
        for b in range(3):
            matrix[a, :, b, :] = (float(a == b) / length + r[..., a] * r[..., b] / length**3) / (8.0 * np.pi)
    return matrix.reshape(3 * count, 3 * count)


def mirror_basis(points, signs):
    count = len(points)
    place = {tuple(np.round(p * (ORDER - 1)).astype(int)): i for i, p in enumerate(points)}
    corner = [i for i, p in enumerate(points) if (p > 0).all()]
    basis = np.zeros((3 * count, 3 * len(corner)))
    for a in range(3):
        for h, i in enumerate(corner):
            for flip in itertools.product([1, -1], repeat=3):
                j = place[tuple(np.round(points[i] * np.array(flip) * (ORDER - 1)).astype(int))]
                sign = 1
                for axis in range(3):
                    if flip[axis] == -1:
                        sign *= signs[axis] * (-1 if axis == a else 1)
                basis[a * count + j, a * len(corner) + h] = sign
    return basis / np.sqrt(8.0)


@functools.lru_cache(maxsize=1)
def tables():
    points = surface_points()
    kernels = {o: kernel_matrix(points, o) for o in ALL_OFFSETS}
    stacked = np.concatenate([kernels[o] for o in ALL_OFFSETS], axis=1)
    basis = np.zeros((DENS, 512))
    sign_y = np.ones(512)
    high, low, main = [], [], []
    for t, (sx, sz) in enumerate([(1, 1), (-1, 1), (1, -1), (-1, -1)]):
        found = []
        for sy in (1, -1):
            mirror = mirror_basis(points, (sx, sy, sz))
            left, size, _ = np.linalg.svd(mirror.T @ stacked, full_matrices=False)
            for j in range(left.shape[1]):
                found.append((size[j], sy, rounded(mirror @ left[:, j])))
        found.sort(key=lambda item: -item[0])
        start = 128 * t + 32 * t
        special = range(start, start + 2 * TOP)
        rest = [lane for lane in range(128 * t, 128 * t + 128) if lane not in special]
        for j, (_, sy, column) in enumerate(found):
            lane = start + j if j < TOP else rest[j - TOP]
            basis[:, lane] = column
            sign_y[lane] = sy
            main.append(lane)
            if j < TOP:
                high.append(lane)
                low.append(lane + TOP)
                sign_y[lane + TOP] = sy
    inverse = np.linalg.inv(basis[:, main])
    doubled = basis.copy()
    doubled[:, low] = basis[:, high]
    special = np.zeros((DENS, 128))
    for t in range(4):
        special[:, 32 * t : 32 * t + 2 * TOP] = doubled[:, 160 * t : 160 * t + 2 * TOP]
    weights = np.zeros((2, COUNT, 256, 256), ml_dtypes.bfloat16)
    for k, offset in enumerate(EVEN_OFFSETS):
        core = np.zeros((512, 512))
        core[np.ix_(main, main)] = (inverse @ kernels[offset] @ inverse.T).T
        leading = core[np.ix_(high, high)]
        core[np.ix_(low, high)] = leading
        core[np.ix_(high, low)] = leading - rounded(leading)
        weights[0, k] = core[:256, :256].astype(ml_dtypes.bfloat16)
        weights[1, k] = core[256:, 256:].astype(ml_dtypes.bfloat16)
    picks = np.zeros((2, 2, len(ALL_OFFSETS), 128), ml_dtypes.bfloat16)
    for cx in range(2):
        for cy in range(2):
            for k, (a, b) in enumerate(EVEN_OFFSETS):
                offset = (-a if cx else a, -b if cy else b)
                picks[cx, cy, ALL_OFFSETS.index(offset), k] = 1
    return {
        "weights": weights.reshape(2, COUNT * 256, 256),
        "doubled": doubled.astype(ml_dtypes.bfloat16),
        "special": special.astype(ml_dtypes.bfloat16),
        "doubled_t": np.ascontiguousarray(doubled.T).astype(ml_dtypes.bfloat16),
        "special_t": np.ascontiguousarray(special.T).astype(ml_dtypes.bfloat16),
        "sign_y": np.tile(sign_y[None, :], (8, 1)).astype(np.float32),
        "picks": picks,
    }


def split(value):
    high = value.astype(BF16)
    return high, (value - high.astype(F32)).astype(BF16)


def mm(a, b):
    return jnp.dot(a, b, preferred_element_type=F32)


def mm_t(a, b):
    return lax.dot_general(a, b, (((1,), (1,)), ((), ())), preferred_element_type=F32)


def product(rows, high_matrix, low_matrix):
    count = rows.shape[0]
    high, low = split(rows)
    both = mm_t(jnp.concatenate([high, low], axis=0), high_matrix)
    return both[:count] + both[count:] + mm_t(high, low_matrix)


def lanes(t):
    return slice(128 * t, 128 * t + 128)


def lane_index(shape):
    return lax.broadcasted_iota(jnp.int32, shape, len(shape) - 1)


def project(rows, doubled, special):
    high, low = split(rows)
    main = mm(high, doubled)
    fine = mm(low, special)
    place = lane_index(fine.shape)
    tiles = []
    for t in range(4):
        tile = main[:, lanes(t)]
        tile = jnp.where((place >= 32 * t) & (place < 32 * t + 32), tile + fine, tile)
        left_over = tile - tile.astype(BF16).astype(F32)
        tiles.append(jnp.where((place >= 32 * t + TOP) & (place < 32 * t + 2 * TOP), left_over, tile))
    return jnp.concatenate(tiles, axis=1)


def expand(y, doubled_t, special_t):
    high = y.astype(BF16)
    rest = y - high.astype(F32)
    place = lane_index((y.shape[0], 128))
    fine = jnp.zeros((y.shape[0], 128), F32)
    for t in range(4):
        fine = jnp.where((place >= 32 * t) & (place < 32 * t + 32), rest[:, lanes(t)], fine)
    return mm(high, doubled_t) + mm(fine.astype(BF16), special_t)


def turned(shape):
    return jnp.where(lax.rem(lax.div(lane_index(shape), 128), 2) == 1, -1.0, 1.0)


DIRECTIONS = [(0, -1), (0, 1), (-1, -1), (-1, 1), (1, -1), (1, 1), (-1, 0), (1, 0)]

SENDS = (2, 3, 4, 5, 0, 1, 6, 7)


def pack_sides(row_of, strips, corners, rows, width):
    half = rows // 2
    for side in range(2):
        for col in range(2):
            y = (width - 2 if side else 0) + col
            for parity in range(2):
                for i in range(half):
                    at = col * rows + parity * half + i
                    strips[side, at : at + 1, :] = row_of(2 * i + parity, y)
    for sx in range(2):
        for sy in range(2):
            for col in range(2):
                y = (width - 2 if sy else 0) + col
                for parity in range(2):
                    x = (rows - 2 if sx else 0) + parity
                    at = 2 * col + parity
                    corners[sx, sy, at : at + 1, :] = row_of(x, y)


def side_copies(block, strips, corners, got_x, got_y, got_c, send, recv, rows, ids):
    copies = []
    for n, (dx, dy) in enumerate(DIRECTIONS):
        sx, sy = (dx + 1) // 2, (dy + 1) // 2
        if dy == 0:
            source = block.at[rows - 2 : rows] if dx > 0 else block.at[0:2]
            target = got_x.at[1 - sx]
        elif dx == 0:
            source, target = strips.at[sy], got_y.at[1 - sy]
        else:
            source, target = corners.at[sx, sy], got_c.at[1 - sx, 1 - sy]
        copies.append(
            pltpu.make_async_remote_copy(
                src_ref=source,
                dst_ref=target,
                send_sem=send.at[n],
                recv_sem=recv.at[n],
                device_id=ids[n],
                device_id_type=MESH,
            )
        )
    return copies


def finish(copies, n):
    dx, dy = DIRECTIONS[n]
    copies[n].wait_send()
    copies[DIRECTIONS.index((-dx, -dy))].wait_recv()


def project_sides(got_x, got_y, got_c, doubled, special):
    parts = [got_x[...].reshape(-1, DENS)] if got_x is not None else []
    parts += [got_y[...].reshape(-1, DENS)]
    parts += [got_c[sx, sy] for sx in range(2) for sy in range(2)]
    return project(jnp.concatenate(parts, axis=0), doubled, special)


def place_sides(put, held, first, rows):
    half = rows // 2
    for side in range(2):
        for col in range(2):
            for parity in range(2):
                for i in range(half):
                    at = first + (side * 2 + col) * rows + parity * half + i
                    put(parity, 1 + i, side, col, held[at : at + 1, :])
                for sx in range(2):
                    at = first + 4 * rows + (sx * 2 + side) * 4 + 2 * col + parity
                    put(parity, (half + 1) * sx, side, col, held[at : at + 1, :])


def fill_leaf(padded, children, doubled, special, rows, chunk):
    half = rows // 2
    places = children.shape[2]
    for c in range(0, half, chunk):
        value = children[2 * c : 2 * c + 2 * chunk].reshape(4 * chunk * places, DENS)
        value = project(value, doubled, special).reshape(chunk, 2, 2, places, 512)
        for parity in range(2):
            padded[parity, 1 + c : 1 + c + chunk, :, 8 : 8 + places, :] = value[:, parity]


def fill_leaf_x(padded, got_x, doubled, special, rows, places):
    half = rows // 2
    value = project(got_x[...].reshape(8 * places, DENS), doubled, special).reshape(2, 2, places, 2, 512)
    for side in range(2):
        for parity in range(2):
            for cy in range(2):
                padded[parity, (half + 1) * side, cy, 8 : 8 + places, :] = value[side, parity, :, cy]


def fill_leaf_y(padded, held, rows, places):
    def put(parity, x, side, col, row):
        y = 8 + places if side else 7
        padded[parity, x, col, y : y + 1, :] = row

    place_sides(put, held, 0, rows)


def shift_leaf(padded, shifted, sign_y, places, steps):
    signs = sign_y[0:1, :].reshape(1, 1, 512)
    for step in steps:
        d = step + 2
        for parity in range(2):
            found = []
            for target in range(2):
                source = target + (-step if target else step)
                start = 8 + source // 2
                value = padded[parity, :, source % 2, start : start + places, :]
                found.append(value * signs if target else value)
            shifted[d, parity] = jnp.concatenate(found, axis=1).astype(BF16)


def fill_parent(padded, block, doubled, special, rows, width):
    half = rows // 2
    value = project(block[...].reshape(rows * width, DENS), doubled, special).reshape(half, 2, width, 512)
    for parity in range(2):
        padded[parity, 1 : 1 + half, 8 : 8 + width, :] = value[:, parity]
    zero = jnp.zeros((half + 2, 8, 512), F32)
    for parity in range(2):
        padded[parity, :, 0:8, :] = zero
        padded[parity, :, 8 + width : 16 + width, :] = zero


def fill_parent_sides(padded, held, rows, width):
    half = rows // 2
    value = held[0 : 4 * width, :].reshape(2, 2, width, 512)
    for side in range(2):
        for parity in range(2):
            padded[parity, (half + 1) * side, 8 : 8 + width, :] = value[side, parity]

    def put(parity, x, side, col, row):
        y = 8 + width + col if side else 6 + col
        padded[parity, x, y : y + 1, :] = row

    place_sides(put, held, 4 * width, rows)


def shift_parent(padded, shifted, sign_y, width):
    row = lax.broadcasted_iota(jnp.int32, (padded.shape[1], width, 512), 1)
    even = lax.rem(row, 2) == 0
    signs = sign_y[0:1, :].reshape(1, 1, 512)
    for d in range(6):
        step = d - 2
        for parity in range(2):
            forward = padded[parity, :, 8 + step : 8 + step + width, :]
            backward = padded[parity, :, 8 - step : 8 - step + width, :] * signs
            shifted[d, parity] = jnp.where(even, forward, backward)


def leaf_flags(lists, picks, rows, width):
    half, places = rows // 2, width // 2
    block = lists[...].astype(F32).reshape(half, 2, places, 2, len(ALL_OFFSETS))
    found = []
    for cx in range(2):
        pair = []
        for cy in range(2):
            part = block[:, cx, :, cy, :].reshape(half * places, len(ALL_OFFSETS)).astype(BF16)
            pair.append(mm(part, picks[cx, cy]).reshape(half, places, 128))
        found.append(jnp.concatenate(pair, axis=1))
    return found


def parent_flags(lists, picks, rows, width):
    half = rows // 2
    block = lists[...].astype(F32).reshape(half, 2, width, len(ALL_OFFSETS))
    even = lax.rem(lax.broadcasted_iota(jnp.int32, (half, width, 128), 1), 2) == 0
    found = []
    for cx in range(2):
        part = block[:, cx].reshape(half * width, len(ALL_OFFSETS)).astype(BF16)
        pair = [mm(part, picks[cx, cy]).reshape(half, width, 128) for cy in range(2)]
        found.append(jnp.where(even, pair[0], pair[1]))
    return found


GROUPS = [tuple(range(first, first + 3)) for first in range(0, COUNT, 3)]


def block_pieces(shifted, flags, half, width, k):
    a, b = EVEN_OFFSETS[k]
    pieces = [[] for _ in range(4)]
    for cx in range(2):
        source = cx + (-a if cx else a)
        parity, start = source % 2, source // 2 + 1
        flag = jnp.broadcast_to(flags[cx, :, :, k : k + 1], (half, width, 128)).astype(shifted.dtype)
        for t in range(4):
            mask = -flag if (cx and t % 2) else flag
            piece = shifted[b + 2, parity, start : start + half, :, lanes(t)] * mask
            pieces[t].append(piece.reshape(half * width, 128).astype(BF16))
    return [jnp.concatenate(piece, axis=0) for piece in pieces]


def interact(group, weights, levels):
    parts = [[], []]
    for k in group:
        found = [level[0](k) for level in levels]
        for t in range(4):
            parts[t // 2].append(jnp.concatenate([one[t] for one in found], axis=0))
    for z in range(2):
        rows = slice(256 * group[0], 256 * group[-1] + 256)
        term = mm(jnp.concatenate(parts[z], axis=1), weights[z, rows, :])
        cols = slice(256 * z, 256 * z + 256)
        at = 0
        for _, count, total, first in levels:
            if first:
                total[:, cols] = term[at : at + count]
            else:
                total[:, cols] += term[at : at + count]
            at += count


def near_body(
    sizes,
    leaf_hbm, parent_in_hbm, leaf_lists_hbm, parent_lists_hbm, up_hbm, down_hbm, inverse_hbm,
    weights_hbm, doubled_hbm, special_hbm, doubled_t_hbm, special_t_hbm, sign_hbm, picks_hbm,
    leaf_check, parent_up, inverse_high, inverse_low,
    leaf, parent_in, leaf_lists, parent_lists, up, down, inverse,
    weights, doubled, special, doubled_t, special_t, sign_y, picks,
    down_high, down_low,
    leaf_strips, leaf_corners, leaf_got_x, leaf_got_y, leaf_got_c, leaf_held,
    parent_strips, parent_corners, parent_got_x, parent_got_y, parent_got_c, parent_held,
    children, leaf_padded, leaf_shifted, leaf_marks,
    parent_padded, parent_shifted, parent_marks, parent_local, leaf_total, parent_total,
    load_sem, leaf_send, leaf_recv, parent_send, parent_recv,
):
    rows, width, prows, pwidth, gx_size, gy_size = sizes
    half, phalf = rows // 2, prows // 2
    places = width // 2
    pairs = [(leaf_hbm, leaf)]
    pairs += [(up_hbm.at[c], up.at[c]) for c in range(4)]
    pairs += [(doubled_hbm, doubled), (special_hbm, special), (sign_hbm, sign_y), (picks_hbm, picks)]
    pairs += [(leaf_lists_hbm, leaf_lists), (parent_lists_hbm, parent_lists)]
    pairs += [(down_hbm, down), (inverse_hbm, inverse), (weights_hbm, weights)]
    pairs += [(doubled_t_hbm, doubled_t), (special_t_hbm, special_t), (parent_in_hbm, parent_in)]
    loads = [pltpu.make_async_copy(a, b, load_sem.at[n]) for n, (a, b) in enumerate(pairs)]
    for load in loads:
        load.start()

    gx, gy = lax.axis_index("gx"), lax.axis_index("gy")
    ids = [
        (lax.rem(gx + dx + gx_size, gx_size), lax.rem(gy + dy + gy_size, gy_size)) for dx, dy in DIRECTIONS
    ]
    barrier = pltpu.get_barrier_semaphore()
    inside = [
        (gx + dx >= 0) & (gx + dx < gx_size) & (gy + dy >= 0) & (gy + dy < gy_size) for dx, dy in DIRECTIONS
    ]
    count = sum(here.astype(jnp.int32) for here in inside)

    def each(action, turns=tuple(range(len(DIRECTIONS)))):
        for n in turns:
            pl.when(inside[n])(functools.partial(action, n))

    for got in (leaf_got_x, leaf_got_y, leaf_got_c, parent_got_x, parent_got_y, parent_got_c):
        got[...] = jnp.zeros_like(got)
    each(lambda n: pl.semaphore_signal(barrier, inc=1, device_id=ids[n], device_id_type=MESH))

    loads[0].wait()
    pack_sides(lambda x, y: leaf[x, y : y + 1, :], leaf_strips, leaf_corners, rows, width)
    pl.semaphore_wait(barrier, count)
    leaf_copies = side_copies(
        leaf, leaf_strips, leaf_corners, leaf_got_x, leaf_got_y, leaf_got_c, leaf_send, leaf_recv, rows, ids
    )
    each(lambda n: leaf_copies[n].start(), SENDS)
    for cy in range(2):
        children[:, cy] = leaf[...].reshape(rows, places, 2, DENS)[:, :, cy, :]
    for c in range(4):
        loads[1 + c].wait()
        child = children[...].reshape(prows, 2, 2, pwidth, DENS)[:, c // 2, c % 2].reshape(prows * pwidth, DENS)
        term = product(child, *split(up[c])).reshape(prows, pwidth, DENS)
        if c == 0:
            parent_up[...] = term
        else:
            parent_up[...] += term
    pack_sides(lambda x, y: parent_up[x, y : y + 1, :], parent_strips, parent_corners, prows, pwidth)
    parent_copies = side_copies(
        parent_up, parent_strips, parent_corners, parent_got_x, parent_got_y, parent_got_c,
        parent_send, parent_recv, prows, ids,
    )
    each(lambda n: parent_copies[n].start(), SENDS)

    for load in loads[5:13]:
        load.wait()
    basis = (doubled[...], special[...])
    fill_leaf(leaf_padded, children, *basis, rows, 3)
    fill_parent(parent_padded, parent_up, *basis, prows, pwidth)
    for cx, value in enumerate(leaf_flags(leaf_lists, picks, rows, width)):
        leaf_marks[cx] = value
    for cx, value in enumerate(parent_flags(parent_lists, picks, prows, pwidth)):
        parent_marks[cx] = value
    for load in loads[13:]:
        load.wait()
    each(functools.partial(finish, leaf_copies), (6, 7))
    fill_leaf_x(leaf_padded, leaf_got_x, *basis, rows, places)
    shift_leaf(leaf_padded, leaf_shifted, sign_y, places, (0, 1))
    leaf_pieces = functools.partial(block_pieces, leaf_shifted, leaf_marks, half, width)
    for group in GROUPS[3:5]:
        interact(group, weights, [(leaf_pieces, rows * width, leaf_total, group == GROUPS[3])])

    each(functools.partial(finish, leaf_copies), tuple(range(6)))
    leaf_held[...] = project_sides(None, leaf_got_y, leaf_got_c, *basis)
    fill_leaf_y(leaf_padded, leaf_held, rows, places)
    shift_leaf(leaf_padded, leaf_shifted, sign_y, places, (-2, -1, 2, 3))
    each(functools.partial(finish, parent_copies))
    parent_held[...] = project_sides(parent_got_x, parent_got_y, parent_got_c, *basis)
    fill_parent_sides(parent_padded, parent_held, prows, pwidth)
    shift_parent(parent_padded, parent_shifted, sign_y, pwidth)
    parent_pieces = functools.partial(block_pieces, parent_shifted, parent_marks, phalf, pwidth)
    for turn, group in enumerate(GROUPS[:3] + GROUPS[5:]):
        levels = [(leaf_pieces, rows * width, leaf_total, False)]
        interact(group, weights, levels + [(parent_pieces, prows * pwidth, parent_total, turn == 0)])
        if turn < 4:
            down_high[turn], down_low[turn] = split(down[turn])
        elif turn == 4:
            inverse_high[...], inverse_low[...] = split(inverse[...])
    for group in GROUPS[3:5]:
        interact(group, weights, [(parent_pieces, prows * pwidth, parent_total, False)])

    signs = sign_y[0:1, :].reshape(1, 1, 512)
    leaf_count, parent_count = rows * width, prows * pwidth
    y = parent_total[...].reshape(2, phalf, pwidth, 512)
    row = lax.broadcasted_iota(jnp.int32, (phalf, pwidth, 512), 1)
    y = [jnp.where(lax.rem(row, 2) == 0, part, part * signs) for part in (y[0], y[1] * turned((1, 1, 512)))]
    y = jnp.concatenate(y, axis=0).reshape(parent_count, 512)
    value = product(expand(y, doubled_t[...], special_t[...]), inverse_high[...], inverse_low[...])
    value = value.reshape(2, phalf, pwidth, DENS)
    for cx in range(2):
        for i in range(phalf):
            parent_local[2 * i + cx] = value[cx, i] + parent_in[2 * i + cx]

    quarter = leaf_count // 4
    for c in range(4):
        y = leaf_total[c * quarter : (c + 1) * quarter, :].reshape(half // 2, 2, places, 512)
        if c >= 2:
            y = y * turned((1, 1, 1, 512))
        y = jnp.concatenate([y[:, 0:1], y[:, 1:2] * signs.reshape(1, 1, 1, 512)], axis=1).reshape(quarter, 512)
        value = expand(y, doubled_t[...], special_t[...]).reshape(half // 2, 2, places, DENS)
        for i in range(half // 2):
            leaf_check[2 * (i + (c % 2) * (half // 2)) + c // 2] = value[i]

    local = parent_local[...].reshape(parent_count, DENS)
    for c in range(4):
        value = product(local, down_high[c], down_low[c]).reshape(prows, pwidth, DENS)
        for i in range(prows):
            leaf_check[2 * i + c // 2, c % 2] += value[i]


def last_body(check, parent_up, high, low, leaf_down_hbm, parent_up_hbm, leaf_down, sem):
    rows, _, places, _ = check.shape
    copies = [pltpu.make_async_copy(parent_up, parent_up_hbm, sem.at[0])]
    copies[0].start()
    part = rows // 2
    for c in range(2):
        here = slice(part * c, part * c + part)
        value = product(check[here].reshape(part * 2 * places, DENS), high[...], low[...])
        value = value.reshape(part, 2, places, DENS)
        pair = [value[:, cy].reshape(part, places, 1, DENS) for cy in range(2)]
        leaf_down[here] = jnp.concatenate(pair, axis=2).reshape(part, 2 * places, DENS)
        copies.append(pltpu.make_async_copy(leaf_down.at[here], leaf_down_hbm.at[here], sem.at[1 + c]))
        copies[-1].start()
    for copy in copies:
        copy.wait()


def local(sizes, leaf_up, parent_in, leaf_lists, parent_lists, up_transfer, down_transfer, check_inverse):
    rows, width, prows, pwidth = sizes[:4]
    half, phalf = rows // 2, prows // 2
    places = width // 2
    names = ("weights", "doubled", "special", "doubled_t", "special_t", "sign_y", "picks")
    constants = [jnp.asarray(tables()[name]) for name in names]
    operands = [leaf_up, parent_in, leaf_lists, parent_lists, up_transfer, down_transfer, check_inverse] + constants
    scratch = [pltpu.VMEM(x.shape, x.dtype) for x in operands]
    scratch += [pltpu.VMEM((4, DENS, DENS), BF16)] * 2

    def sides(x_shape, rows_here, total):
        return [
            pltpu.VMEM((2, 2 * rows_here, DENS), F32),
            pltpu.VMEM((2, 2, 4, DENS), F32),
            pltpu.VMEM((2, 2) + x_shape + (DENS,), F32),
            pltpu.VMEM((2, 2 * rows_here, DENS), F32),
            pltpu.VMEM((2, 2, 4, DENS), F32),
            pltpu.VMEM((total, 512), F32),
        ]

    scratch += sides((width,), rows, 4 * rows + 16)
    scratch += sides((pwidth,), prows, 4 * pwidth + 4 * prows + 16)
    scratch += [
        pltpu.VMEM((rows, 2, places, DENS), F32),
        pltpu.VMEM((2, half + 2, 2, 16 + places, 512), F32),
        pltpu.VMEM((6, 2, half + 2, width, 512), BF16),
        pltpu.VMEM((2, half, width, 128), F32),
        pltpu.VMEM((2, phalf + 2, 16 + pwidth, 512), F32),
        pltpu.VMEM((6, 2, phalf + 2, pwidth, 512), F32),
        pltpu.VMEM((2, phalf, pwidth, 128), F32),
        pltpu.VMEM((prows, pwidth, DENS), F32),
        pltpu.VMEM((rows * width, 512), F32),
        pltpu.VMEM((prows * pwidth, 512), F32),
        pltpu.SemaphoreType.DMA((17,)),
        pltpu.SemaphoreType.DMA((8,)),
        pltpu.SemaphoreType.DMA((8,)),
        pltpu.SemaphoreType.DMA((8,)),
        pltpu.SemaphoreType.DMA((8,)),
    ]
    check, parent_up, high, low = pl.pallas_call(
        functools.partial(near_body, sizes),
        out_shape=(
            pltpu.VMEM((rows, 2, places, DENS), F32),
            pltpu.VMEM((prows, pwidth, DENS), F32),
            pltpu.VMEM((DENS, DENS), BF16),
            pltpu.VMEM((DENS, DENS), BF16),
        ),
        in_specs=[pl.BlockSpec(memory_space=pltpu.HBM)] * len(operands),
        out_specs=(pl.BlockSpec(memory_space=pltpu.VMEM),) * 4,
        scratch_shapes=scratch,
        compiler_params=pltpu.CompilerParams(
            collective_id=0, has_side_effects=True, vmem_limit_bytes=60 * 1024 * 1024
        ),
    )(*operands)
    return pl.pallas_call(
        last_body,
        out_shape=(
            jax.ShapeDtypeStruct((rows, width, DENS), F32),
            jax.ShapeDtypeStruct((prows, pwidth, DENS), F32),
        ),
        in_specs=[pl.BlockSpec(memory_space=pltpu.VMEM)] * 4,
        out_specs=(pl.BlockSpec(memory_space=pltpu.HBM),) * 2,
        scratch_shapes=[pltpu.VMEM((rows, width, DENS), F32), pltpu.SemaphoreType.DMA((3,))],
        compiler_params=pltpu.CompilerParams(vmem_limit_bytes=16 * 1024 * 1024),
    )(check, parent_up, high, low)


def solution(mesh):
    gx_size, gy_size = mesh.shape["gx"], mesh.shape["gy"]
    sizes = (192 // gx_size, 256 // gy_size, 96 // gx_size, 128 // gy_size, gx_size, gy_size)
    placed = (P("gx", "gy", None),) * 4 + (P(), P(), P())
    return jax.shard_map(
        functools.partial(local, sizes),
        mesh=mesh,
        in_specs=placed,
        out_specs=(P("gx", "gy", None), P("gx", "gy", None)),
        check_vma=False,
    )
```

```python
import functools
import itertools

import jax
import jax.numpy as jnp
import ml_dtypes
import numpy as np
from jax import lax
from jax.experimental import pallas as pl
from jax.experimental.pallas import tpu as pltpu
from jax.sharding import PartitionSpec as P

ORDER = 6
DENS = 456
TOP = 14
F32 = jnp.float32
BF16 = jnp.bfloat16
MESH = pl.DeviceIdType.MESH

ALL_OFFSETS = [(a, b) for a in range(-3, 4) for b in range(-3, 4) if max(abs(a), abs(b)) >= 2]
EVEN_OFFSETS = [
    (a, b)
    for steps in ((-2, -1), (0, 1), (2, 3))
    for a in range(-2, 4)
    for b in steps
    if max(abs(a), abs(b)) >= 2
]
COUNT = len(EVEN_OFFSETS)


def rounded(values):
    return values.astype(ml_dtypes.bfloat16).astype(np.float64)


def surface_points():
    grid_line = np.linspace(-1.0, 1.0, ORDER)
    points = []
    for i in range(ORDER):
        for j in range(ORDER):
            for k in range(ORDER):
                if min(i, j, k) == 0 or max(i, j, k) == ORDER - 1:
                    points.append((grid_line[i], grid_line[j], grid_line[k]))
    return np.array(points)


def kernel_matrix(points, shift):
    r = 0.525 * (points[:, None, :] - points[None, :, :]) - np.array([shift[0], shift[1], 0.0])
    length = np.sqrt((r * r).sum(-1))
    count = len(points)
    matrix = np.zeros((3, count, 3, count))
    for a in range(3):
        for b in range(3):
            matrix[a, :, b, :] = (float(a == b) / length + r[..., a] * r[..., b] / length**3) / (8.0 * np.pi)
    return matrix.reshape(3 * count, 3 * count)


def mirror_basis(points, signs):
    count = len(points)
    place = {tuple(np.round(p * (ORDER - 1)).astype(int)): i for i, p in enumerate(points)}
    corner = [i for i, p in enumerate(points) if (p > 0).all()]
    basis = np.zeros((3 * count, 3 * len(corner)))
    for a in range(3):
        for h, i in enumerate(corner):
            for flip in itertools.product([1, -1], repeat=3):
                j = place[tuple(np.round(points[i] * np.array(flip) * (ORDER - 1)).astype(int))]
                sign = 1
                for axis in range(3):
                    if flip[axis] == -1:
                        sign *= signs[axis] * (-1 if axis == a else 1)
                basis[a * count + j, a * len(corner) + h] = sign
    return basis / np.sqrt(8.0)


@functools.lru_cache(maxsize=1)
def tables():
    points = surface_points()
    kernels = {o: kernel_matrix(points, o) for o in ALL_OFFSETS}
    stacked = np.concatenate([kernels[o] for o in ALL_OFFSETS], axis=1)
    basis = np.zeros((DENS, 512))
    sign_y = np.ones(512)
    high, low, main = [], [], []
    for t, (sx, sz) in enumerate([(1, 1), (-1, 1), (1, -1), (-1, -1)]):
        found = []
        for sy in (1, -1):
            mirror = mirror_basis(points, (sx, sy, sz))
            left, size, _ = np.linalg.svd(mirror.T @ stacked, full_matrices=False)
            for j in range(left.shape[1]):
                found.append((size[j], sy, rounded(mirror @ left[:, j])))
        found.sort(key=lambda item: -item[0])
        start = 128 * t + 32 * t
        special = range(start, start + 2 * TOP)
        rest = [lane for lane in range(128 * t, 128 * t + 128) if lane not in special]
        for j, (_, sy, column) in enumerate(found):
            lane = start + j if j < TOP else rest[j - TOP]
            basis[:, lane] = column
            sign_y[lane] = sy
            main.append(lane)
            if j < TOP:
                high.append(lane)
                low.append(lane + TOP)
                sign_y[lane + TOP] = sy
    inverse = np.linalg.inv(basis[:, main])
    doubled = basis.copy()
    doubled[:, low] = basis[:, high]
    special = np.zeros((DENS, 128))
    for t in range(4):
        special[:, 32 * t : 32 * t + 2 * TOP] = doubled[:, 160 * t : 160 * t + 2 * TOP]
    weights = np.zeros((2, COUNT, 256, 256), ml_dtypes.bfloat16)
    for k, offset in enumerate(EVEN_OFFSETS):
        core = np.zeros((512, 512))
        core[np.ix_(main, main)] = (inverse @ kernels[offset] @ inverse.T).T
        leading = core[np.ix_(high, high)]
        core[np.ix_(low, high)] = leading
        core[np.ix_(high, low)] = leading - rounded(leading)
        weights[0, k] = core[:256, :256].astype(ml_dtypes.bfloat16)
        weights[1, k] = core[256:, 256:].astype(ml_dtypes.bfloat16)
    picks = np.zeros((2, 2, len(ALL_OFFSETS), 128), ml_dtypes.bfloat16)
    for cx in range(2):
        for cy in range(2):
            for k, (a, b) in enumerate(EVEN_OFFSETS):
                offset = (-a if cx else a, -b if cy else b)
                picks[cx, cy, ALL_OFFSETS.index(offset), k] = 1
    return {
        "weights": weights.reshape(2, COUNT * 256, 256),
        "doubled": doubled.astype(ml_dtypes.bfloat16),
        "special": special.astype(ml_dtypes.bfloat16),
        "doubled_t": np.ascontiguousarray(doubled.T).astype(ml_dtypes.bfloat16),
        "special_t": np.ascontiguousarray(special.T).astype(ml_dtypes.bfloat16),
        "sign_y": np.tile(sign_y[None, :], (8, 1)).astype(np.float32),
        "picks": picks,
    }


def split(value):
    high = value.astype(BF16)
    return high, (value - high.astype(F32)).astype(BF16)


def mm(a, b):
    return jnp.dot(a, b, preferred_element_type=F32)


def mm_t(a, b):
    return lax.dot_general(a, b, (((1,), (1,)), ((), ())), preferred_element_type=F32)


def product(rows, high_matrix, low_matrix):
    count = rows.shape[0]
    high, low = split(rows)
    both = mm_t(jnp.concatenate([high, low], axis=0), high_matrix)
    return both[:count] + both[count:] + mm_t(high, low_matrix)


def lanes(t):
    return slice(128 * t, 128 * t + 128)


def lane_index(shape):
    return lax.broadcasted_iota(jnp.int32, shape, len(shape) - 1)


def project(rows, doubled, special):
    high, low = split(rows)
    main = mm(high, doubled)
    fine = mm(low, special)
    place = lane_index(fine.shape)
    tiles = []
    for t in range(4):
        tile = main[:, lanes(t)]
        tile = jnp.where((place >= 32 * t) & (place < 32 * t + 32), tile + fine, tile)
        left_over = tile - tile.astype(BF16).astype(F32)
        tiles.append(jnp.where((place >= 32 * t + TOP) & (place < 32 * t + 2 * TOP), left_over, tile))
    return jnp.concatenate(tiles, axis=1)


def expand(y, doubled_t, special_t):
    high = y.astype(BF16)
    rest = y - high.astype(F32)
    place = lane_index((y.shape[0], 128))
    fine = jnp.zeros((y.shape[0], 128), F32)
    for t in range(4):
        fine = jnp.where((place >= 32 * t) & (place < 32 * t + 32), rest[:, lanes(t)], fine)
    return mm(high, doubled_t) + mm(fine.astype(BF16), special_t)


def turned(shape):
    return jnp.where(lax.rem(lax.div(lane_index(shape), 128), 2) == 1, -1.0, 1.0)


DIRECTIONS = [(0, -1), (0, 1), (-1, -1), (-1, 1), (1, -1), (1, 1), (-1, 0), (1, 0)]

SENDS = (2, 3, 4, 5, 0, 1, 6, 7)


def pack_sides(row_of, strips, corners, rows, width):
    half = rows // 2
    for side in range(2):
        for col in range(2):
            y = (width - 2 if side else 0) + col
            for parity in range(2):
                for i in range(half):
                    at = col * rows + parity * half + i
                    strips[side, at : at + 1, :] = row_of(2 * i + parity, y)
    for sx in range(2):
        for sy in range(2):
            for col in range(2):
                y = (width - 2 if sy else 0) + col
                for parity in range(2):
                    x = (rows - 2 if sx else 0) + parity
                    at = 2 * col + parity
                    corners[sx, sy, at : at + 1, :] = row_of(x, y)


def side_copies(block, strips, corners, got_x, got_y, got_c, send, recv, rows, ids):
    copies = []
    for n, (dx, dy) in enumerate(DIRECTIONS):
        sx, sy = (dx + 1) // 2, (dy + 1) // 2
        if dy == 0:
            source = block.at[rows - 2 : rows] if dx > 0 else block.at[0:2]
            target = got_x.at[1 - sx]
        elif dx == 0:
            source, target = strips.at[sy], got_y.at[1 - sy]
        else:
            source, target = corners.at[sx, sy], got_c.at[1 - sx, 1 - sy]
        copies.append(
            pltpu.make_async_remote_copy(
                src_ref=source,
                dst_ref=target,
                send_sem=send.at[n],
                recv_sem=recv.at[n],
                device_id=ids[n],
                device_id_type=MESH,
            )
        )
    return copies


def finish(copies, n):
    dx, dy = DIRECTIONS[n]
    copies[n].wait_send()
    copies[DIRECTIONS.index((-dx, -dy))].wait_recv()


def project_sides(got_x, got_y, got_c, doubled, special):
    parts = [got_x[...].reshape(-1, DENS)] if got_x is not None else []
    parts += [got_y[...].reshape(-1, DENS)]
    parts += [got_c[sx, sy] for sx in range(2) for sy in range(2)]
    return project(jnp.concatenate(parts, axis=0), doubled, special)


def place_sides(put, held, first, rows):
    half = rows // 2
    for side in range(2):
        for col in range(2):
            for parity in range(2):
                for i in range(half):
                    at = first + (side * 2 + col) * rows + parity * half + i
                    put(parity, 1 + i, side, col, held[at : at + 1, :])
                for sx in range(2):
                    at = first + 4 * rows + (sx * 2 + side) * 4 + 2 * col + parity
                    put(parity, (half + 1) * sx, side, col, held[at : at + 1, :])


def fill_leaf(padded, children, doubled, special, rows, chunk):
    half = rows // 2
    places = children.shape[2]
    for c in range(0, half, chunk):
        value = children[2 * c : 2 * c + 2 * chunk].reshape(4 * chunk * places, DENS)
        value = project(value, doubled, special).reshape(chunk, 2, 2, places, 512)
        for parity in range(2):
            padded[parity, 1 + c : 1 + c + chunk, :, 8 : 8 + places, :] = value[:, parity]


def fill_leaf_x(padded, got_x, doubled, special, rows, places):
    half = rows // 2
    value = project(got_x[...].reshape(8 * places, DENS), doubled, special).reshape(2, 2, places, 2, 512)
    for side in range(2):
        for parity in range(2):
            for cy in range(2):
                padded[parity, (half + 1) * side, cy, 8 : 8 + places, :] = value[side, parity, :, cy]


def fill_leaf_y(padded, held, rows, places):
    def put(parity, x, side, col, row):
        y = 8 + places if side else 7
        padded[parity, x, col, y : y + 1, :] = row

    place_sides(put, held, 0, rows)


def shift_leaf(padded, shifted, sign_y, places, steps):
    signs = sign_y[0:1, :].reshape(1, 1, 512)
    for step in steps:
        d = step + 2
        for parity in range(2):
            found = []
            for target in range(2):
                source = target + (-step if target else step)
                start = 8 + source // 2
                value = padded[parity, :, source % 2, start : start + places, :]
                found.append(value * signs if target else value)
            shifted[d, parity] = jnp.concatenate(found, axis=1).astype(BF16)


def fill_parent(padded, block, doubled, special, rows, width):
    half = rows // 2
    value = project(block[...].reshape(rows * width, DENS), doubled, special).reshape(half, 2, width, 512)
    for parity in range(2):
        padded[parity, 1 : 1 + half, 8 : 8 + width, :] = value[:, parity]
    zero = jnp.zeros((half + 2, 8, 512), F32)
    for parity in range(2):
        padded[parity, :, 0:8, :] = zero
        padded[parity, :, 8 + width : 16 + width, :] = zero


def fill_parent_sides(padded, held, rows, width):
    half = rows // 2
    value = held[0 : 4 * width, :].reshape(2, 2, width, 512)
    for side in range(2):
        for parity in range(2):
            padded[parity, (half + 1) * side, 8 : 8 + width, :] = value[side, parity]

    def put(parity, x, side, col, row):
        y = 8 + width + col if side else 6 + col
        padded[parity, x, y : y + 1, :] = row

    place_sides(put, held, 4 * width, rows)


def shift_parent(padded, shifted, sign_y, width):
    row = lax.broadcasted_iota(jnp.int32, (padded.shape[1], width, 512), 1)
    even = lax.rem(row, 2) == 0
    signs = sign_y[0:1, :].reshape(1, 1, 512)
    for d in range(6):
        step = d - 2
        for parity in range(2):
            forward = padded[parity, :, 8 + step : 8 + step + width, :]
            backward = padded[parity, :, 8 - step : 8 - step + width, :] * signs
            shifted[d, parity] = jnp.where(even, forward, backward)


def leaf_flags(lists, picks, rows, width):
    half, places = rows // 2, width // 2
    block = lists[...].astype(F32).reshape(half, 2, places, 2, len(ALL_OFFSETS))
    found = []
    for cx in range(2):
        pair = []
        for cy in range(2):
            part = block[:, cx, :, cy, :].reshape(half * places, len(ALL_OFFSETS)).astype(BF16)
            pair.append(mm(part, picks[cx, cy]).reshape(half, places, 128))
        found.append(jnp.concatenate(pair, axis=1))
    return found


def parent_flags(lists, picks, rows, width):
    half = rows // 2
    block = lists[...].astype(F32).reshape(half, 2, width, len(ALL_OFFSETS))
    even = lax.rem(lax.broadcasted_iota(jnp.int32, (half, width, 128), 1), 2) == 0
    found = []
    for cx in range(2):
        part = block[:, cx].reshape(half * width, len(ALL_OFFSETS)).astype(BF16)
        pair = [mm(part, picks[cx, cy]).reshape(half, width, 128) for cy in range(2)]
        found.append(jnp.where(even, pair[0], pair[1]))
    return found


GROUPS = [tuple(range(first, first + 3)) for first in range(0, COUNT, 3)]


def block_pieces(shifted, flags, half, width, k):
    a, b = EVEN_OFFSETS[k]
    pieces = [[] for _ in range(4)]
    for cx in range(2):
        source = cx + (-a if cx else a)
        parity, start = source % 2, source // 2 + 1
        flag = jnp.broadcast_to(flags[cx, :, :, k : k + 1], (half, width, 128)).astype(shifted.dtype)
        for t in range(4):
            mask = -flag if (cx and t % 2) else flag
            piece = shifted[b + 2, parity, start : start + half, :, lanes(t)] * mask
            pieces[t].append(piece.reshape(half * width, 128).astype(BF16))
    return [jnp.concatenate(piece, axis=0) for piece in pieces]


def interact(group, weights, levels):
    parts = [[], []]
    for k in group:
        found = [level[0](k) for level in levels]
        for t in range(4):
            parts[t // 2].append(jnp.concatenate([one[t] for one in found], axis=0))
    for z in range(2):
        rows = slice(256 * group[0], 256 * group[-1] + 256)
        term = mm(jnp.concatenate(parts[z], axis=1), weights[z, rows, :])
        cols = slice(256 * z, 256 * z + 256)
        at = 0
        for _, count, total, first in levels:
            if first:
                total[:, cols] = term[at : at + count]
            else:
                total[:, cols] += term[at : at + count]
            at += count


def near_body(
    sizes,
    leaf_hbm, parent_in_hbm, leaf_lists_hbm, parent_lists_hbm, up_hbm, down_hbm, inverse_hbm,
    weights_hbm, doubled_hbm, special_hbm, doubled_t_hbm, special_t_hbm, sign_hbm, picks_hbm,
    leaf_check, parent_up, inverse_high, inverse_low,
    leaf, parent_in, leaf_lists, parent_lists, up, down, inverse,
    weights, doubled, special, doubled_t, special_t, sign_y, picks,
    down_high, down_low,
    leaf_strips, leaf_corners, leaf_got_x, leaf_got_y, leaf_got_c, leaf_held,
    parent_strips, parent_corners, parent_got_x, parent_got_y, parent_got_c, parent_held,
    children, leaf_padded, leaf_shifted, leaf_marks,
    parent_padded, parent_shifted, parent_marks, parent_local, leaf_total, parent_total,
    load_sem, leaf_send, leaf_recv, parent_send, parent_recv,
):
    rows, width, prows, pwidth, gx_size, gy_size = sizes
    half, phalf = rows // 2, prows // 2
    places = width // 2
    pairs = [(leaf_hbm, leaf)]
    pairs += [(up_hbm.at[c], up.at[c]) for c in range(4)]
    pairs += [(doubled_hbm, doubled), (special_hbm, special), (sign_hbm, sign_y), (picks_hbm, picks)]
    pairs += [(leaf_lists_hbm, leaf_lists), (parent_lists_hbm, parent_lists)]
    pairs += [(down_hbm, down), (inverse_hbm, inverse), (weights_hbm, weights)]
    pairs += [(doubled_t_hbm, doubled_t), (special_t_hbm, special_t), (parent_in_hbm, parent_in)]
    loads = [pltpu.make_async_copy(a, b, load_sem.at[n]) for n, (a, b) in enumerate(pairs)]
    for load in loads:
        load.start()

    gx, gy = lax.axis_index("gx"), lax.axis_index("gy")
    ids = [
        (lax.rem(gx + dx + gx_size, gx_size), lax.rem(gy + dy + gy_size, gy_size)) for dx, dy in DIRECTIONS
    ]
    barrier = pltpu.get_barrier_semaphore()
    inside = [
        (gx + dx >= 0) & (gx + dx < gx_size) & (gy + dy >= 0) & (gy + dy < gy_size) for dx, dy in DIRECTIONS
    ]
    count = sum(here.astype(jnp.int32) for here in inside)

    def each(action, turns=tuple(range(len(DIRECTIONS)))):
        for n in turns:
            pl.when(inside[n])(functools.partial(action, n))

    for got in (leaf_got_x, leaf_got_y, leaf_got_c, parent_got_x, parent_got_y, parent_got_c):
        got[...] = jnp.zeros_like(got)
    each(lambda n: pl.semaphore_signal(barrier, inc=1, device_id=ids[n], device_id_type=MESH))

    loads[0].wait()
    pack_sides(lambda x, y: leaf[x, y : y + 1, :], leaf_strips, leaf_corners, rows, width)
    pl.semaphore_wait(barrier, count)
    leaf_copies = side_copies(
        leaf, leaf_strips, leaf_corners, leaf_got_x, leaf_got_y, leaf_got_c, leaf_send, leaf_recv, rows, ids
    )
    each(lambda n: leaf_copies[n].start(), SENDS)
    for cy in range(2):
        children[:, cy] = leaf[...].reshape(rows, places, 2, DENS)[:, :, cy, :]
    for c in range(4):
        loads[1 + c].wait()
        child = children[...].reshape(prows, 2, 2, pwidth, DENS)[:, c // 2, c % 2].reshape(prows * pwidth, DENS)
        term = product(child, *split(up[c])).reshape(prows, pwidth, DENS)
        if c == 0:
            parent_up[...] = term
        else:
            parent_up[...] += term
    pack_sides(lambda x, y: parent_up[x, y : y + 1, :], parent_strips, parent_corners, prows, pwidth)
    parent_copies = side_copies(
        parent_up, parent_strips, parent_corners, parent_got_x, parent_got_y, parent_got_c,
        parent_send, parent_recv, prows, ids,
    )
    each(lambda n: parent_copies[n].start(), SENDS)

    for load in loads[5:13]:
        load.wait()
    basis = (doubled[...], special[...])
    fill_leaf(leaf_padded, children, *basis, rows, 3)
    fill_parent(parent_padded, parent_up, *basis, prows, pwidth)
    for cx, value in enumerate(leaf_flags(leaf_lists, picks, rows, width)):
        leaf_marks[cx] = value
    for cx, value in enumerate(parent_flags(parent_lists, picks, prows, pwidth)):
        parent_marks[cx] = value
    for load in loads[13:]:
        load.wait()
    each(functools.partial(finish, leaf_copies), (6, 7))
    fill_leaf_x(leaf_padded, leaf_got_x, *basis, rows, places)
    shift_leaf(leaf_padded, leaf_shifted, sign_y, places, (0, 1))
    leaf_pieces = functools.partial(block_pieces, leaf_shifted, leaf_marks, half, width)
    for group in GROUPS[3:5]:
        interact(group, weights, [(leaf_pieces, rows * width, leaf_total, group == GROUPS[3])])
    for c in range(4):
        down_high[c], down_low[c] = split(down[c])
    inverse_high[...], inverse_low[...] = split(inverse[...])

    each(functools.partial(finish, leaf_copies), tuple(range(6)))
    leaf_held[...] = project_sides(None, leaf_got_y, leaf_got_c, *basis)
    fill_leaf_y(leaf_padded, leaf_held, rows, places)
    shift_leaf(leaf_padded, leaf_shifted, sign_y, places, (-2, -1, 2, 3))
    each(functools.partial(finish, parent_copies))
    parent_held[...] = project_sides(parent_got_x, parent_got_y, parent_got_c, *basis)
    fill_parent_sides(parent_padded, parent_held, prows, pwidth)
    shift_parent(parent_padded, parent_shifted, sign_y, pwidth)
    parent_pieces = functools.partial(block_pieces, parent_shifted, parent_marks, phalf, pwidth)
    for turn, group in enumerate(GROUPS[:3] + GROUPS[5:]):
        levels = [(leaf_pieces, rows * width, leaf_total, False)]
        interact(group, weights, levels + [(parent_pieces, prows * pwidth, parent_total, turn == 0)])
    for group in GROUPS[3:5]:
        interact(group, weights, [(parent_pieces, prows * pwidth, parent_total, False)])

    signs = sign_y[0:1, :].reshape(1, 1, 512)
    leaf_count, parent_count = rows * width, prows * pwidth
    y = parent_total[...].reshape(2, phalf, pwidth, 512)
    row = lax.broadcasted_iota(jnp.int32, (phalf, pwidth, 512), 1)
    y = [jnp.where(lax.rem(row, 2) == 0, part, part * signs) for part in (y[0], y[1] * turned((1, 1, 512)))]
    y = jnp.concatenate(y, axis=0).reshape(parent_count, 512)
    value = product(expand(y, doubled_t[...], special_t[...]), inverse_high[...], inverse_low[...])
    value = value.reshape(2, phalf, pwidth, DENS)
    for cx in range(2):
        for i in range(phalf):
            parent_local[2 * i + cx] = value[cx, i] + parent_in[2 * i + cx]

    quarter = leaf_count // 4
    for c in range(4):
        y = leaf_total[c * quarter : (c + 1) * quarter, :].reshape(half // 2, 2, places, 512)
        if c >= 2:
            y = y * turned((1, 1, 1, 512))
        y = jnp.concatenate([y[:, 0:1], y[:, 1:2] * signs.reshape(1, 1, 1, 512)], axis=1).reshape(quarter, 512)
        value = expand(y, doubled_t[...], special_t[...]).reshape(half // 2, 2, places, DENS)
        for i in range(half // 2):
            leaf_check[2 * (i + (c % 2) * (half // 2)) + c // 2] = value[i]

    local = parent_local[...].reshape(parent_count, DENS)
    for c in range(4):
        value = product(local, down_high[c], down_low[c]).reshape(prows, pwidth, DENS)
        for i in range(prows):
            leaf_check[2 * i + c // 2, c % 2] += value[i]


def last_body(check, parent_up, high, low, leaf_down_hbm, parent_up_hbm, leaf_down, sem):
    rows, _, places, _ = check.shape
    copies = [pltpu.make_async_copy(parent_up, parent_up_hbm, sem.at[0])]
    copies[0].start()
    part = rows // 2
    for c in range(2):
        here = slice(part * c, part * c + part)
        value = product(check[here].reshape(part * 2 * places, DENS), high[...], low[...])
        value = value.reshape(part, 2, places, DENS)
        pair = [value[:, cy].reshape(part, places, 1, DENS) for cy in range(2)]
        leaf_down[here] = jnp.concatenate(pair, axis=2).reshape(part, 2 * places, DENS)
        copies.append(pltpu.make_async_copy(leaf_down.at[here], leaf_down_hbm.at[here], sem.at[1 + c]))
        copies[-1].start()
    for copy in copies:
        copy.wait()


def local(sizes, leaf_up, parent_in, leaf_lists, parent_lists, up_transfer, down_transfer, check_inverse):
    rows, width, prows, pwidth = sizes[:4]
    half, phalf = rows // 2, prows // 2
    places = width // 2
    names = ("weights", "doubled", "special", "doubled_t", "special_t", "sign_y", "picks")
    constants = [jnp.asarray(tables()[name]) for name in names]
    operands = [leaf_up, parent_in, leaf_lists, parent_lists, up_transfer, down_transfer, check_inverse] + constants
    scratch = [pltpu.VMEM(x.shape, x.dtype) for x in operands]
    scratch += [pltpu.VMEM((4, DENS, DENS), BF16)] * 2

    def sides(x_shape, rows_here, total):
        return [
            pltpu.VMEM((2, 2 * rows_here, DENS), F32),
            pltpu.VMEM((2, 2, 4, DENS), F32),
            pltpu.VMEM((2, 2) + x_shape + (DENS,), F32),
            pltpu.VMEM((2, 2 * rows_here, DENS), F32),
            pltpu.VMEM((2, 2, 4, DENS), F32),
            pltpu.VMEM((total, 512), F32),
        ]

    scratch += sides((width,), rows, 4 * rows + 16)
    scratch += sides((pwidth,), prows, 4 * pwidth + 4 * prows + 16)
    scratch += [
        pltpu.VMEM((rows, 2, places, DENS), F32),
        pltpu.VMEM((2, half + 2, 2, 16 + places, 512), F32),
        pltpu.VMEM((6, 2, half + 2, width, 512), BF16),
        pltpu.VMEM((2, half, width, 128), F32),
        pltpu.VMEM((2, phalf + 2, 16 + pwidth, 512), F32),
        pltpu.VMEM((6, 2, phalf + 2, pwidth, 512), F32),
        pltpu.VMEM((2, phalf, pwidth, 128), F32),
        pltpu.VMEM((prows, pwidth, DENS), F32),
        pltpu.VMEM((rows * width, 512), F32),
        pltpu.VMEM((prows * pwidth, 512), F32),
        pltpu.SemaphoreType.DMA((17,)),
        pltpu.SemaphoreType.DMA((8,)),
        pltpu.SemaphoreType.DMA((8,)),
        pltpu.SemaphoreType.DMA((8,)),
        pltpu.SemaphoreType.DMA((8,)),
    ]
    check, parent_up, high, low = pl.pallas_call(
        functools.partial(near_body, sizes),
        out_shape=(
            pltpu.VMEM((rows, 2, places, DENS), F32),
            pltpu.VMEM((prows, pwidth, DENS), F32),
            pltpu.VMEM((DENS, DENS), BF16),
            pltpu.VMEM((DENS, DENS), BF16),
        ),
        in_specs=[pl.BlockSpec(memory_space=pltpu.HBM)] * len(operands),
        out_specs=(pl.BlockSpec(memory_space=pltpu.VMEM),) * 4,
        scratch_shapes=scratch,
        compiler_params=pltpu.CompilerParams(
            collective_id=0, has_side_effects=True, vmem_limit_bytes=60 * 1024 * 1024
        ),
    )(*operands)
    return pl.pallas_call(
        last_body,
        out_shape=(
            jax.ShapeDtypeStruct((rows, width, DENS), F32),
            jax.ShapeDtypeStruct((prows, pwidth, DENS), F32),
        ),
        in_specs=[pl.BlockSpec(memory_space=pltpu.VMEM)] * 4,
        out_specs=(pl.BlockSpec(memory_space=pltpu.HBM),) * 2,
        scratch_shapes=[pltpu.VMEM((rows, width, DENS), F32), pltpu.SemaphoreType.DMA((3,))],
        compiler_params=pltpu.CompilerParams(vmem_limit_bytes=16 * 1024 * 1024),
    )(check, parent_up, high, low)


def solution(mesh):
    gx_size, gy_size = mesh.shape["gx"], mesh.shape["gy"]
    sizes = (192 // gx_size, 256 // gy_size, 96 // gx_size, 128 // gy_size, gx_size, gy_size)
    placed = (P("gx", "gy", None),) * 4 + (P(), P(), P())
    return jax.shard_map(
        functools.partial(local, sizes),
        mesh=mesh,
        in_specs=placed,
        out_specs=(P("gx", "gy", None), P("gx", "gy", None)),
        check_vma=False,
    )
```
